32 devices in a mesh: blk: 4 (over y, x), dp: 8 (over z, core).
Axes of the slice: x: 2, y: 2, z: 4, core: 2. Of those that a mesh axis runs over, the one named last changes fastest.
Arguments:
- queries: bfloat16 [4096, 4096], P(('blk', 'dp')), may hold values from -6 to 6
- passages: bfloat16 [4096, 4096], P(('blk', 'dp')), may hold values from -6 to 6
- hard_ids: int32 [4096, 8], P(('blk', 'dp')), may hold values from 0 to 1023, as said below
- query_weight: float32 [4096], P(('blk', 'dp')), may hold values from 4 to 40
Outputs:
- query_grads: float32 [4096, 4096], P(('blk', 'dp'))
- passage_grads: float32 [4096, 4096], P(('blk', 'dp'))
- mean_loss: float32 [], replicated
The draws below stay inside these ranges and needn't reach their ends.
Inputs may be any that keep to these rules, and one draw needn't show every extreme that they name: `hard_ids`: of the 1024 ids of one device's queries, at most 192 have the same value of id // 128, and in every device's block some value has exactly 192.
All inputs are finite; a program needn't handle non-finite values.
Results may differ from the reference program's by a relative error of at most 0.0034.
Values may be sent and summed in bfloat16 or wider, within the bound.
A program may use at most 192 MiB of HBM per device.

```python
import math
import jax
import jax.numpy as jnp
from jax import lax

D = 4096
QRY_DEV = 128
HARD = 8
CAP = 192
QUERIES = 4096
N_BLK = 4
N_DP = 8


def normal_passages(key):
    passage_key = jax.random.fold_in(key, 7)
    return jnp.clip(jax.random.normal(passage_key, (QUERIES, D), jnp.float32), -6.0, 6.0)


def hard_id_table(key):
    key = jax.random.fold_in(key, 5)
    slot_count = N_DP * CAP
    wanted_count = HARD * QRY_DEV

    def one_device(device_key):
        first_key, second_key, third_key, fourth_key = jax.random.split(device_key, 4)
        priority = jax.random.permutation(first_key, slot_count).astype(jnp.int32)
        full_owner = jax.random.randint(second_key, (), 0, N_DP)
        slot_index = jnp.arange(slot_count, dtype=jnp.int32)
        priority = jnp.where(slot_index // CAP == full_owner, slot_index - slot_count, priority)
        chosen = jnp.argsort(priority)[:wanted_count].astype(jnp.int32)
        owners = jax.random.permutation(third_key, chosen // CAP)
        rows_local = jax.random.randint(fourth_key, (wanted_count,), 0, QRY_DEV)
        return (owners * QRY_DEV + rows_local).astype(jnp.int32).reshape(QRY_DEV, HARD)
    device_keys = jax.random.split(key, QUERIES // QRY_DEV)
    return jax.vmap(one_device)(device_keys).reshape(QUERIES, HARD)


def pooled_negatives(key, values):
    id_table = hard_id_table(key)
    pool_span = N_DP * QRY_DEV
    row_base = jnp.arange(QUERIES, dtype=jnp.int32) // pool_span * pool_span
    total = jnp.zeros((QUERIES, D), jnp.float32)
    for slot in range(HARD):
        total = total + values[row_base + id_table[:, slot]]
    return total


def draw_hard_ids(key, part):
    return hard_id_table(key)


def draw_passages(key, part):
    values = normal_passages(key)
    return values.astype(jnp.bfloat16)


def draw_queries(key, part):
    level = math.log(N_BLK * QRY_DEV / HARD)
    passage_vals = normal_passages(key)
    pulled = pooled_negatives(key, passage_vals)
    key = jax.random.fold_in(key, 3)
    noise = 0.5 * jax.random.normal(key, (QUERIES, D), jnp.float32)
    factor = (level + 1.0) / (4.0 * math.sqrt(D))
    values = jnp.clip(factor * pulled + noise, -6.0, 6.0)
    return values.astype(jnp.bfloat16)


def block_scale(key, shape, cuts, least, top_value):
    def one(dim, shards_of):
        steps = jax.random.uniform(jax.random.fold_in(jax.random.fold_in(key, 6), dim), (shards_of,), jnp.float32, least / len(cuts), top_value / len(cuts))
        return jnp.repeat(jnp.exp(steps), shape[dim] // shards_of).reshape((-1,) + (1,) * (len(shape) - dim - 1))

    level = one(*cuts[0])
    for cut in cuts[1:]:
        level = level * one(*cut)
    return level


def setup_inputs(seed: int = 0) -> dict:
    seeds = jax.random.split(jax.random.key(seed), 5)
    queries = draw_queries(jax.random.fold_in(seeds[4], 71), 0)
    passages = draw_passages(jax.random.fold_in(seeds[4], 71), 0)
    hard_ids = draw_hard_ids(jax.random.fold_in(seeds[4], 71), 0)
    query_weight = jnp.clip(jnp.exp(math.log(40.0) - 2.3025851 * jax.random.uniform(seeds[3], (QUERIES,), jnp.float32) ** block_scale(seeds[3], (QUERIES,), ((0, 32),), -0.2, 0.2)), 4.0, 40.0)
    return {"queries": queries, "passages": passages, "hard_ids": hard_ids, "query_weight": query_weight}


def reference(queries, passages, hard_ids, query_weight):
    rescale = 4.0 / math.sqrt(D)
    query_four = queries.reshape(N_BLK, N_DP, QRY_DEV, D)
    passage_four = passages.reshape(N_BLK, N_DP, QRY_DEV, D)
    ids_three = hard_ids.reshape(N_BLK, N_DP, QRY_DEV, HARD)
    weight_three = query_weight.reshape(N_BLK, N_DP, QRY_DEV)
    local_rows = jnp.arange(QRY_DEV, dtype=jnp.int32)
    tile_cols = jnp.arange(N_BLK * QRY_DEV, dtype=jnp.int32)

    def device_step(accum, block):
        blk_index = block // N_DP
        dp_index = block % N_DP
        query_rows = query_four[blk_index, dp_index]
        weights = weight_three[blk_index, dp_index]
        id_rows = ids_three[blk_index, dp_index]
        group_rows = passage_four[:, dp_index].reshape(N_BLK * QRY_DEV, D)
        pool_rows = passage_four[blk_index].reshape(N_DP * QRY_DEV, D)
        negatives = pool_rows[id_rows]
        logits = jnp.dot(query_rows, group_rows.T, preferred_element_type=jnp.float32) * rescale
        hard_logits = jnp.einsum('rd,rkd->rk', query_rows.astype(jnp.float32), negatives.astype(jnp.float32)) * rescale
        highest = jnp.maximum(lax.optimization_barrier(jnp.max(logits, axis=1)), lax.optimization_barrier(jnp.max(hard_logits, axis=1)))
        sumexp = lax.optimization_barrier(jnp.sum(jnp.exp(logits - highest[:, None]), axis=1)) + lax.optimization_barrier(jnp.sum(jnp.exp(hard_logits - highest[:, None]), axis=1))
        lse = highest + jnp.log(sumexp)
        own_cols = (blk_index * QRY_DEV + local_rows).astype(jnp.int32)
        positive = jnp.take_along_axis(logits, own_cols[:, None], axis=1)[:, 0]
        loss_term = jnp.sum(weights * (lse - positive))
        coefs = rescale * weights
        positive_mask = (tile_cols[None, :] == own_cols[:, None]).astype(jnp.float32)
        tile_coef = (coefs[:, None] * (jnp.exp(logits - lse[:, None]) - positive_mask)).astype(jnp.bfloat16)
        hard_coef = (coefs[:, None] * jnp.exp(hard_logits - lse[:, None])).astype(jnp.bfloat16)
        grad_rows = jnp.dot(tile_coef, group_rows, preferred_element_type=jnp.float32)
        grad_rows = grad_rows + jnp.einsum('rk,rkd->rd', hard_coef.astype(jnp.float32), negatives.astype(jnp.float32))
        tile_term = jnp.dot(tile_coef.T, query_rows, preferred_element_type=jnp.float32)
        hard_terms = (hard_coef[:, :, None] * query_rows[:, None, :]).astype(jnp.bfloat16)
        pool_term = jnp.zeros((N_DP * QRY_DEV, D), jnp.float32).at[id_rows.reshape(-1)].add(hard_terms.reshape(-1, D).astype(jnp.float32))
        accum = accum.at[:, dp_index].add(tile_term.reshape(N_BLK, QRY_DEV, D))
        accum = accum.at[blk_index].add(pool_term.reshape(N_DP, QRY_DEV, D))
        return (accum, (grad_rows, loss_term))
    start = jnp.zeros((N_BLK, N_DP, QRY_DEV, D), jnp.float32)
    accum, (grad_blocks, loss_terms) = lax.scan(device_step, start, jnp.arange(N_BLK * N_DP, dtype=jnp.int32))
    query_grads = grad_blocks.reshape(QUERIES, D)
    passage_grads = accum.reshape(QUERIES, D)
    mean_loss = jnp.sum(loss_terms) / QUERIES
    return (query_grads, passage_grads, mean_loss)
```

```python
import math

import jax
import jax.numpy as jnp
from jax import lax
from jax.sharding import PartitionSpec as P


def pooled(queries, passages, hard_ids, query_weight):
    rows_dev = queries.shape[0]
    width = queries.shape[1]
    hard_count = hard_ids.shape[1]
    rescale = 4.0 / math.sqrt(width)
    blk_count = lax.axis_size("blk")
    dp_count = lax.axis_size("dp")
    blk_index = lax.axis_index("blk")
    local_rows = jnp.arange(rows_dev, dtype=jnp.int32)
    pool_passages = lax.all_gather(passages, "dp", axis=0, tiled=True)
    group_passages = lax.all_gather(passages, "blk", axis=0, tiled=True)
    pool_queries = lax.all_gather(queries, "dp", axis=0, tiled=True)
    group_queries = lax.all_gather(queries, "blk", axis=0, tiled=True)
    contract = (((1,), (1,)), ((), ()))
    tile = lax.dot_general(queries, group_passages, contract, preferred_element_type=jnp.float32)
    tile = tile * rescale
    pool = lax.dot_general(queries, pool_passages, contract, preferred_element_type=jnp.float32)
    pool = pool * rescale
    pool_cols = jnp.arange(dp_count * rows_dev, dtype=jnp.int32)
    times = jnp.zeros(pool.shape, jnp.float32)
    for k in range(hard_count):
        times = times + (hard_ids[:, k : k + 1] == pool_cols[None, :]).astype(jnp.float32)
    taken = jnp.where(times > 0.0, pool, -jnp.inf)
    highest = jnp.maximum(jnp.max(tile, axis=1), jnp.max(taken, axis=1))
    sumexp = jnp.sum(jnp.exp(tile - highest[:, None]), axis=1) + jnp.sum(
        times * jnp.exp(taken - highest[:, None]), axis=1
    )
    lse = highest + jnp.log(sumexp)
    tile_cols = jnp.arange(blk_count * rows_dev, dtype=jnp.int32)
    own = tile_cols[None, :] == (blk_index * rows_dev + local_rows)[:, None]
    positive = jnp.sum(jnp.where(own, tile, 0.0), axis=1)
    loss_part = jnp.sum(query_weight * (lse - positive))
    mean_loss = lax.psum(loss_part, ("blk", "dp")) / (rows_dev * blk_count * dp_count)
    coefs = (rescale * query_weight)[:, None]
    tile_coef = (coefs * (jnp.exp(tile - lse[:, None]) - own.astype(jnp.float32))).astype(
        jnp.bfloat16
    )
    one_coef = (coefs * jnp.exp(taken - lse[:, None])).astype(jnp.bfloat16)
    pool_coef = (times * one_coef.astype(jnp.float32)).astype(jnp.bfloat16)
    query_grads = jnp.dot(tile_coef, group_passages, preferred_element_type=jnp.float32) + jnp.dot(
        pool_coef, pool_passages, preferred_element_type=jnp.float32
    )
    back_tile = lax.all_to_all(
        tile_coef.T.reshape(blk_count, rows_dev, rows_dev), "blk", 0, 0, tiled=True
    )
    back_pool = lax.all_to_all(
        pool_coef.T.reshape(dp_count, rows_dev, rows_dev), "dp", 0, 0, tiled=True
    )
    back_tile = back_tile.transpose(1, 0, 2).reshape(rows_dev, -1)
    back_pool = back_pool.transpose(1, 0, 2).reshape(rows_dev, -1)
    passage_grads = jnp.dot(back_tile, group_queries, preferred_element_type=jnp.float32) + jnp.dot(
        back_pool, pool_queries, preferred_element_type=jnp.float32
    )
    return (query_grads, passage_grads, mean_loss)


def solution(mesh):
    return jax.shard_map(
        pooled,
        mesh=mesh,
        in_specs=(
            P(("blk", "dp"), None),
            P(("blk", "dp"), None),
            P(("blk", "dp"), None),
            P(("blk", "dp")),
        ),
        out_specs=(P(("blk", "dp"), None), P(("blk", "dp"), None), P()),
        check_vma=False,
    )
```

```python
import functools
import math

import jax
import jax.numpy as jnp
from jax import lax
from jax.experimental import pallas as pl
from jax.experimental.pallas import tpu as pltpu
from jax.sharding import PartitionSpec as P


def pooled(queries, passages, hard_ids, query_weight):
    rows_dev = queries.shape[0]
    width = queries.shape[1]
    hard_count = hard_ids.shape[1]
    rescale = 4.0 / math.sqrt(width)
    blk_count = lax.axis_size("blk")
    dp_count = lax.axis_size("dp")
    blk_index = lax.axis_index("blk")
    local_rows = jnp.arange(rows_dev, dtype=jnp.int32)
    pool_passages = lax.all_gather(passages, "dp", axis=0, tiled=True)
    group_passages = lax.all_gather(passages, "blk", axis=0, tiled=True)
    pool_queries = lax.all_gather(queries, "dp", axis=0, tiled=True)
    group_queries = lax.all_gather(queries, "blk", axis=0, tiled=True)
    contract = (((1,), (1,)), ((), ()))
    tile = lax.dot_general(queries, group_passages, contract, preferred_element_type=jnp.float32)
    tile = tile * rescale
    pool = lax.dot_general(queries, pool_passages, contract, preferred_element_type=jnp.float32)
    pool = pool * rescale
    pool_cols = jnp.arange(dp_count * rows_dev, dtype=jnp.int32)
    times = jnp.zeros(pool.shape, jnp.float32)
    for k in range(hard_count):
        times = times + (hard_ids[:, k : k + 1] == pool_cols[None, :]).astype(jnp.float32)
    taken = jnp.where(times > 0.0, pool, -jnp.inf)
    highest = jnp.maximum(jnp.max(tile, axis=1), jnp.max(taken, axis=1))
    sumexp = jnp.sum(jnp.exp(tile - highest[:, None]), axis=1) + jnp.sum(
        times * jnp.exp(taken - highest[:, None]), axis=1
    )
    lse = highest + jnp.log(sumexp)
    tile_cols = jnp.arange(blk_count * rows_dev, dtype=jnp.int32)
    own = tile_cols[None, :] == (blk_index * rows_dev + local_rows)[:, None]
    positive = jnp.sum(jnp.where(own, tile, 0.0), axis=1)
    loss_part = jnp.sum(query_weight * (lse - positive))
    mean_loss = lax.psum(loss_part, ("blk", "dp")) / (rows_dev * blk_count * dp_count)
    coefs = (rescale * query_weight)[:, None]
    tile_coef = (coefs * (jnp.exp(tile - lse[:, None]) - own.astype(jnp.float32))).astype(
        jnp.bfloat16
    )
    one_coef = (coefs * jnp.exp(taken - lse[:, None])).astype(jnp.bfloat16)
    pool_coef = (times * one_coef.astype(jnp.float32)).astype(jnp.bfloat16)
    query_grads = jnp.dot(tile_coef, group_passages, preferred_element_type=jnp.float32) + jnp.dot(
        pool_coef, pool_passages, preferred_element_type=jnp.float32
    )
    back_tile = lax.all_to_all(
        tile_coef.T.reshape(blk_count, rows_dev, rows_dev), "blk", 0, 0, tiled=True
    )
    back_pool = lax.all_to_all(
        pool_coef.T.reshape(dp_count, rows_dev, rows_dev), "dp", 0, 0, tiled=True
    )
    back_tile = back_tile.transpose(1, 0, 2).reshape(rows_dev, -1)
    back_pool = back_pool.transpose(1, 0, 2).reshape(rows_dev, -1)
    passage_grads = jnp.dot(back_tile, group_queries, preferred_element_type=jnp.float32) + jnp.dot(
        back_pool, pool_queries, preferred_element_type=jnp.float32
    )
    return (query_grads, passage_grads, mean_loss)


MESH = pl.DeviceIdType.MESH
HALVES = 2
CHUNKS = 8
AHEAD = 3
FIRST = 5


def line_kernel(
    blk_count,
    q_ref,
    p_ref,
    ids_ref,
    weight_ref,
    qg_ref,
    pg_ref,
    loss_ref,
    pp,
    pq,
    gp,
    gq,
    r_out,
    r_in,
    lp,
    lt,
    times,
    pc,
    tc,
    ct,
    tt,
    cr,
    ce,
    tr,
    loss_dp,
    loss_blk,
    s_pin,
    s_pout,
    s_psib,
    r_p,
    r_psib,
    s_qin,
    s_qsib,
    r_q,
    r_qsib,
    s_r,
    r_r,
    s_gp,
    r_gp,
    s_gq,
    r_gq,
    s_c,
    r_c,
    r_e,
    s_t,
    r_t,
    s_ld,
    r_ld,
    s_lb,
    r_lb,
):
    b = lax.axis_index("blk")
    d = lax.axis_index("dp")
    rows, width = q_ref.shape
    half = rows // HALVES
    part = width // CHUNKS
    hard_count = ids_ref.shape[1]
    rescale = 4.0 / math.sqrt(width)
    f32, bf16 = jnp.float32, jnp.bfloat16
    z = lax.div(d, 2)
    c = lax.rem(d, 2)
    o = 1 - c
    side = lax.div(z, 2)
    se, sm = 3 * side, 1 + side
    mp, ep = 3 - sm, 3 - se
    sib = (b, 2 * z + o)
    inner = (b, 2 * jnp.where(z == se, sm, mp) + c)
    outer = (b, 2 * se + c)

    barrier = pltpu.get_barrier_semaphore()
    peers = [(b, lax.rem(d + i, 8)) for i in range(1, 8)]
    others = [lax.rem(b + i, blk_count) for i in range(1, blk_count)]
    peers += [(other, d) for other in others]
    for peer in peers:
        pl.semaphore_signal(barrier, inc=1, device_id=peer, device_id_type=MESH)

    def core_rows(core):
        return pl.ds(pl.multiple_of(core * rows, rows), rows)

    pp[z, core_rows(c), :] = p_ref[...]
    pq[z, core_rows(c), :] = q_ref[...]
    gp[core_rows(b), :] = p_ref[...]
    gq[core_rows(b), :] = q_ref[...]
    pl.semaphore_wait(barrier, len(peers))

    def remote(src, dst, send_sem, recv_sem, device):
        return pltpu.make_async_remote_copy(
            src_ref=src,
            dst_ref=dst,
            send_sem=send_sem,
            recv_sem=recv_sem,
            device_id=device,
            device_id_type=MESH,
        )

    def p_slot(zz, core, h):
        return pp.at[zz, pl.ds(pl.multiple_of(core * rows + h * half, half), half), :]

    def q_slot(zz, core, j):
        return pq.at[zz, core_rows(core), pl.ds(j * part, part)]

    def p_src(zz, h, own):
        return p_ref.at[pl.ds(h * half, half), :] if own else p_slot(zz, c, h)

    def q_src(zz, j, own):
        return q_ref.at[:, pl.ds(j * part, part)] if own else q_slot(zz, c, j)

    def p_in(zz, h, own=False):
        return remote(p_src(zz, h, own), p_slot(zz, c, h), s_pin.at[zz, h], r_p.at[zz, h], inner)

    def p_out(zz, h, own=False):
        return remote(p_src(zz, h, own), p_slot(zz, c, h), s_pout.at[zz, h], r_p.at[zz, h], outer)

    def p_sib(zz, h, own=False):
        return remote(p_src(zz, h, own), p_slot(zz, c, h), s_psib.at[zz, h], r_psib.at[zz, h], sib)

    def q_in(zz, j, own=False):
        return remote(q_src(zz, j, own), q_slot(zz, c, j), s_qin.at[zz, j], r_q.at[zz, j], inner)

    def q_sib(zz, j, own=False):
        return remote(q_src(zz, j, own), q_slot(zz, c, j), s_qsib.at[zz, j], r_qsib.at[zz, j], sib)

    def wait_p(zz, h):
        slot = p_slot(zz, c, h)
        remote(slot, slot, s_pin.at[zz, h], r_p.at[zz, h], inner).wait_recv()

    def wait_psib(zz):
        for h in range(HALVES):
            slot = p_slot(zz, o, h)
            remote(slot, slot, s_psib.at[zz, h], r_psib.at[zz, h], sib).wait_recv()

    def wait_q(zz, j):
        slot = q_slot(zz, c, j)
        remote(slot, slot, s_qin.at[zz, j], r_q.at[zz, j], inner).wait_recv()

    def wait_qsib(zz, j):
        slot = q_slot(zz, o, j)
        remote(slot, slot, s_qsib.at[zz, j], r_qsib.at[zz, j], sib).wait_recv()

    def r_copy(j):
        cols = pl.ds(j * part, part)
        return remote(r_out.at[:, cols], r_in.at[:, cols], s_r.at[j], r_r.at[j], outer)

    def gp_copy(i):
        return remote(p_ref, gp.at[core_rows(b), :], s_gp.at[i], r_gp.at[b], (others[i], d))

    def gq_copy(i):
        return remote(q_ref, gq.at[core_rows(b), :], s_gq.at[i], r_gq.at[b], (others[i], d))

    def t_copy(i):
        return remote(
            tt.at[others[i]], tr.at[:, core_rows(b)], s_t.at[i], r_t.at[b], (others[i], d)
        )

    def ld_copy(i):
        return remote(loss_dp.at[d], loss_dp.at[d], s_ld.at[i], r_ld.at[d], peers[i])

    def lb_copy(i):
        return remote(loss_blk.at[b], loss_blk.at[b], s_lb.at[i], r_lb.at[b], (others[i], d))

    def wait_gp():
        for i, other in enumerate(others):
            slot = gp.at[core_rows(other), :]
            remote(slot, slot, s_gp.at[i], r_gp.at[other], (other, d)).wait_recv()

    def wait_gq_and_t():
        for i, other in enumerate(others):
            slot = gq.at[core_rows(other), :]
            remote(slot, slot, s_gq.at[i], r_gq.at[other], (other, d)).wait_recv()
            slot = tr.at[:, core_rows(other)]
            remote(slot, slot, s_t.at[i], r_t.at[other], (other, d)).wait_recv()

    def block_of(buf, sender):
        zs, cs = lax.div(sender, 2), lax.rem(sender, 2)
        return buf.at[zs, :, core_rows(cs)]

    def wait_c(sender):
        slot = block_of(cr, sender)
        remote(slot, slot, s_c.at[0], r_c.at[sender], (b, sender)).wait_recv()

    def wait_e(sender):
        slot = block_of(ce, sender)
        remote(slot, slot, s_c.at[0], r_e.at[sender], (b, sender)).wait_recv()

    def c_copy(s, target):
        return remote(ct.at[s], block_of(cr, d), s_c.at[s], r_c.at[d], (b, target))

    def e_copy(s, target):
        return remote(ct.at[s], block_of(ce, d), s_c.at[s], r_e.at[d], (b, target))

    def each_coef(go):
        for s in range(8):
            zs, cs = s // 2, s % 2
            if zs in (1, 2):
                go(s, s, c_copy, cr, None)
            else:
                go(s, s, c_copy, cr, z == zs)
                go(s, 2 * (1 if zs == 0 else 2) + cs, e_copy, ce, z != zs)

    def start_coef(s, target, copy, buf, cond):
        far = d != target
        near = d == target
        if cond is not None:
            far, near = far & cond, near & cond

        @pl.when(far)
        def _():
            copy(s, target).start()

        @pl.when(near)
        def _():
            buf[z, :, core_rows(c)] = ct[s]

    def end_coef(s, target, copy, buf, cond):
        far = d != target
        if cond is not None:
            far = far & cond

        @pl.when(far)
        def _():
            copy(s, target).wait_send()

    nt = (((1,), (1,)), ((), ()))
    step = min(512, width)

    def pool_logits(zz):
        def body(k, acc):
            cols = pl.ds(pl.multiple_of(k * step, step), step)
            return acc + lax.dot_general(
                q_ref[:, cols], pp[zz, :, cols], nt, preferred_element_type=f32
            )

        zero = jnp.zeros((rows, 2 * rows), f32)
        lp[zz] = lax.fori_loop(0, width // step, body, zero) * rescale

    def tile_logits():
        def body(k, acc):
            cols = pl.ds(pl.multiple_of(k * step, step), step)
            return acc + lax.dot_general(
                q_ref[:, cols], gp[:, cols], nt, preferred_element_type=f32
            )

        zero = jnp.zeros((rows, blk_count * rows), f32)
        lt[...] = lax.fori_loop(0, width // step, body, zero) * rescale

    def count_ids():
        for zz in range(4):
            cols = lax.broadcasted_iota(jnp.int32, (rows, 2 * rows), 1) + zz * 2 * rows
            total = jnp.zeros((rows, 2 * rows), f32)
            for k in range(hard_count):
                total += (ids_ref[:, k : k + 1] == cols).astype(f32)
            times[zz] = total

    def softmax():
        tile = lt[...]
        highest = jnp.max(tile, axis=1, keepdims=True)
        for zz in range(4):
            taken = jnp.where(times[zz] > 0.0, lp[zz], -jnp.inf)
            highest = jnp.maximum(highest, jnp.max(taken, axis=1, keepdims=True))
        sumexp = jnp.sum(jnp.exp(tile - highest), axis=1, keepdims=True)
        for zz in range(4):
            taken = jnp.where(times[zz] > 0.0, lp[zz], -jnp.inf)
            sumexp += jnp.sum(times[zz] * jnp.exp(taken - highest), axis=1, keepdims=True)
        lse = highest + jnp.log(sumexp)
        weight = weight_ref[...]
        coefs = rescale * weight
        for zz in range(4):
            taken = jnp.where(times[zz] > 0.0, lp[zz], -jnp.inf)
            one = (coefs * jnp.exp(taken - lse)).astype(bf16).astype(f32)
            many = times[zz] * one
            pc[zz] = many.astype(bf16)
            for core in range(2):
                ct[2 * zz + core] = many[:, core * rows : (core + 1) * rows].T.astype(bf16)
        each_coef(start_coef)
        row = lax.broadcasted_iota(jnp.int32, tile.shape, 0) + b * rows
        own = lax.broadcasted_iota(jnp.int32, tile.shape, 1) == row
        coef = coefs * (jnp.exp(tile - lse) - own.astype(f32))
        tc[...] = coef.astype(bf16)
        for g in range(blk_count):
            tt[g] = coef[:, g * rows : (g + 1) * rows].T.astype(bf16)
        for i in range(len(others)):
            t_copy(i).start()
        tr[:, core_rows(b)] = tt[b]
        positive = jnp.sum(jnp.where(own, tile, 0.0), axis=1, keepdims=True)
        loss = jnp.sum(weight * (lse - positive), axis=0, keepdims=True)
        loss_dp[d] = jnp.broadcast_to(loss, (8, 128))
        for i in range(7):
            ld_copy(i).start()

    def query_grads():
        @pl.loop(0, CHUNKS)
        def _(j):
            cols = pl.ds(pl.multiple_of(j * part, part), part)
            acc = jnp.dot(tc[...], gp[:, cols], preferred_element_type=f32)
            for zz in range(4):
                acc += jnp.dot(pc[zz], pp[zz, :, cols], preferred_element_type=f32)
            qg_ref[:, cols] = acc

    def group():
        wait_gp()
        for i in range(len(others)):
            gq_copy(i).start()
        tile_logits()

    for i in range(len(others)):
        gp_copy(i).start()

    @pl.when(z == sm)
    def _():
        for h in range(HALVES):
            p_in(sm, h, True).start()
            p_out(sm, h, True).start()
            p_sib(sm, h, True).start()
        count_ids()
        wait_psib(sm)
        pool_logits(sm)
        for h in range(HALVES):
            wait_p(se, h)
            p_in(se, h).start()
            p_sib(se, h).start()
            wait_p(mp, h)
            p_out(mp, h).start()
            p_sib(mp, h).start()
        for j in range(CHUNKS):
            q_sib(sm, j, True).start()
        wait_psib(se)
        pool_logits(se)
        wait_psib(mp)
        pool_logits(mp)
        for h in range(HALVES):
            wait_p(ep, h)
            p_out(ep, h).start()
            p_sib(ep, h).start()
        for j in range(AHEAD):
            q_in(sm, j, True).start()
        for j in range(CHUNKS):
            wait_q(se, j)
            if j < AHEAD:
                q_in(se, j).start()
            q_sib(se, j).start()
        group()
        wait_psib(ep)
        pool_logits(ep)
        softmax()
        query_grads()

        def end_grads(j):
            wait_qsib(sm, j)
            wait_qsib(mp, j)
            wait_qsib(ep, j)
            cols = pl.ds(j * part, part)
            acc = jnp.zeros((rows, part), f32)
            for t in range(1, 4):
                zz = lax.rem(se + t, 4)
                acc += jnp.dot(ce[zz], pq[zz, :, cols], preferred_element_type=f32)
            r_out[:, cols] = acc.astype(bf16)
            r_copy(j).start()

        for j in range(CHUNKS):
            wait_q(mp, j)
            q_sib(mp, j).start()
            wait_q(ep, j)
            q_sib(ep, j).start()
            if j + AHEAD < CHUNKS:
                q_in(sm, j + AHEAD, True).start()
                q_in(se, j + AHEAD).start()
            if j == FIRST:
                for t in range(1, 4):
                    for core in range(2):
                        sender = 2 * lax.rem(se + t, 4) + core

                        @pl.when(sender != d)
                        def _():
                            wait_e(sender)

                for i in range(FIRST):
                    end_grads(i)
            if j >= FIRST:
                end_grads(j)
        for j in range(CHUNKS):
            wait_qsib(se, j)
        for i in range(7):
            wait_c(peers[i][1])
        wait_gq_and_t()

        @pl.loop(0, CHUNKS)
        def _(j):
            cols = pl.ds(pl.multiple_of(j * part, part), part)
            acc = jnp.dot(tr[...], gq[:, cols], preferred_element_type=f32)
            for zz in range(4):
                acc += jnp.dot(cr[zz], pq[zz, :, cols], preferred_element_type=f32)
            pg_ref[:, cols] = acc

        for h in range(HALVES):
            p_in(sm, h, True).wait_send()
            p_out(sm, h, True).wait_send()
            p_sib(sm, h, True).wait_send()
            p_in(se, h).wait_send()
            p_sib(se, h).wait_send()
            p_out(mp, h).wait_send()
            p_sib(mp, h).wait_send()
            p_out(ep, h).wait_send()
            p_sib(ep, h).wait_send()
        for j in range(CHUNKS):
            q_in(sm, j, True).wait_send()
            q_in(se, j).wait_send()
            q_sib(sm, j, True).wait_send()
            q_sib(se, j).wait_send()
            q_sib(mp, j).wait_send()
            q_sib(ep, j).wait_send()
            r_copy(j).wait_send()

    @pl.when(z == se)
    def _():
        for h in range(HALVES):
            p_in(se, h, True).start()
            p_sib(se, h, True).start()
        count_ids()
        wait_psib(se)
        pool_logits(se)
        for h in range(HALVES):
            p_in(se, h, True).wait_send()
        for j in range(CHUNKS):
            q_in(se, j, True).start()
            q_sib(se, j, True).start()
        for zz in (sm, mp, ep):
            if zz is ep:
                group()
            for h in range(HALVES):
                wait_p(zz, h)
                p_sib(zz, h).start()
            wait_psib(zz)
            pool_logits(zz)
        softmax()
        query_grads()
        for j in range(CHUNKS):
            wait_qsib(se, j)
        wait_c(2 * z + o)
        wait_gq_and_t()

        @pl.loop(0, CHUNKS)
        def _(j):
            cols = pl.ds(pl.multiple_of(j * part, part), part)
            acc = jnp.dot(tr[...], gq[:, cols], preferred_element_type=f32)
            pg_ref[:, cols] = acc + jnp.dot(cr[se], pq[se, :, cols], preferred_element_type=f32)

        for j in range(CHUNKS):
            cols = pl.ds(j * part, part)
            r_slot = r_in.at[:, cols]
            remote(r_slot, r_slot, s_r.at[j], r_r.at[j], inner).wait_recv()
            pg_ref[:, cols] += r_in[:, cols].astype(f32)
        for h in range(HALVES):
            p_sib(se, h, True).wait_send()
            for zz in (sm, mp, ep):
                p_sib(zz, h).wait_send()
        for j in range(CHUNKS):
            q_in(se, j, True).wait_send()
            q_sib(se, j, True).wait_send()

    for i in range(7):
        peer = peers[i][1]
        slot = loss_dp.at[peer]
        remote(slot, slot, s_ld.at[i], r_ld.at[peer], peers[i]).wait_recv()
    total = loss_dp[0]
    for s in range(1, 8):
        total = total + loss_dp[s]
    loss_blk[b] = total
    for i in range(len(others)):
        lb_copy(i).start()
    for i, other in enumerate(others):
        slot = loss_blk.at[other]
        remote(slot, slot, s_lb.at[i], r_lb.at[other], (other, d)).wait_recv()
    total = loss_blk[0]
    for g in range(1, blk_count):
        total = total + loss_blk[g]
    loss_ref[...] = total / (rows * blk_count * 8)
    each_coef(end_coef)
    for i in range(len(others)):
        gp_copy(i).wait_send()
        gq_copy(i).wait_send()
        t_copy(i).wait_send()
        lb_copy(i).wait_send()
    for i in range(7):
        ld_copy(i).wait_send()


def on_line(queries, passages, hard_ids, query_weight):
    rows, width = queries.shape
    blk_count = lax.axis_size("blk")
    bf16, f32 = jnp.bfloat16, jnp.float32
    dma = pltpu.SemaphoreType.DMA
    vmem = pl.BlockSpec(memory_space=pltpu.VMEM)
    query_grads, passage_grads, loss = pl.pallas_call(
        functools.partial(line_kernel, blk_count),
        out_shape=(
            jax.ShapeDtypeStruct((rows, width), f32),
            jax.ShapeDtypeStruct((rows, width), f32),
            jax.ShapeDtypeStruct((8, 128), f32),
        ),
        in_specs=[vmem] * 4,
        out_specs=(vmem, vmem, vmem),
        scratch_shapes=[
            pltpu.VMEM((4, 2 * rows, width), bf16),
            pltpu.VMEM((4, 2 * rows, width), bf16),
            pltpu.VMEM((blk_count * rows, width), bf16),
            pltpu.VMEM((blk_count * rows, width), bf16),
            pltpu.VMEM((rows, width), bf16),
            pltpu.VMEM((rows, width), bf16),
            pltpu.VMEM((4, rows, 2 * rows), f32),
            pltpu.VMEM((rows, blk_count * rows), f32),
            pltpu.VMEM((4, rows, 2 * rows), f32),
            pltpu.VMEM((4, rows, 2 * rows), bf16),
            pltpu.VMEM((rows, blk_count * rows), bf16),
            pltpu.VMEM((8, rows, rows), bf16),
            pltpu.VMEM((blk_count, rows, rows), bf16),
            pltpu.VMEM((4, rows, 2 * rows), bf16),
            pltpu.VMEM((4, rows, 2 * rows), bf16),
            pltpu.VMEM((rows, blk_count * rows), bf16),
            pltpu.VMEM((8, 8, 128), f32),
            pltpu.VMEM((blk_count, 8, 128), f32),
        ]
        + [dma((4, HALVES))] * 5
        + [dma((4, CHUNKS))] * 4
        + [dma((CHUNKS,))] * 2
        + [dma((blk_count,))] * 4
        + [dma((8,))] * 3
        + [dma((blk_count,))] * 2
        + [dma((8,))] * 2
        + [dma((blk_count,))] * 2,
        compiler_params=pltpu.CompilerParams(
            collective_id=0, has_side_effects=True, vmem_limit_bytes=56 * 1024 * 1024
        ),
    )(queries, passages, hard_ids, query_weight[:, None])
    return (query_grads, passage_grads, loss[0, 0])


def solution(mesh):
    small = mesh.shape["dp"] == 8 and mesh.shape["blk"] <= 4
    return jax.shard_map(
        on_line if small else pooled,
        mesh=mesh,
        in_specs=(
            P(("blk", "dp"), None),
            P(("blk", "dp"), None),
            P(("blk", "dp"), None),
            P(("blk", "dp")),
        ),
        out_specs=(P(("blk", "dp"), None), P(("blk", "dp"), None), P()),
        check_vma=False,
    )
```

```python
import functools
import math

import jax
import jax.numpy as jnp
from jax import lax
from jax.experimental import pallas as pl
from jax.experimental.pallas import tpu as pltpu
from jax.sharding import PartitionSpec as P


def pooled(queries, passages, hard_ids, query_weight):
    rows_dev = queries.shape[0]
    width = queries.shape[1]
    hard_count = hard_ids.shape[1]
    rescale = 4.0 / math.sqrt(width)
    blk_count = lax.axis_size("blk")
    dp_count = lax.axis_size("dp")
    blk_index = lax.axis_index("blk")
    local_rows = jnp.arange(rows_dev, dtype=jnp.int32)
    pool_passages = lax.all_gather(passages, "dp", axis=0, tiled=True)
    group_passages = lax.all_gather(passages, "blk", axis=0, tiled=True)
    pool_queries = lax.all_gather(queries, "dp", axis=0, tiled=True)
    group_queries = lax.all_gather(queries, "blk", axis=0, tiled=True)
    contract = (((1,), (1,)), ((), ()))
    tile = lax.dot_general(queries, group_passages, contract, preferred_element_type=jnp.float32)
    tile = tile * rescale
    pool = lax.dot_general(queries, pool_passages, contract, preferred_element_type=jnp.float32)
    pool = pool * rescale
    pool_cols = jnp.arange(dp_count * rows_dev, dtype=jnp.int32)
    times = jnp.zeros(pool.shape, jnp.float32)
    for k in range(hard_count):
        times = times + (hard_ids[:, k : k + 1] == pool_cols[None, :]).astype(jnp.float32)
    taken = jnp.where(times > 0.0, pool, -jnp.inf)
    highest = jnp.maximum(jnp.max(tile, axis=1), jnp.max(taken, axis=1))
    sumexp = jnp.sum(jnp.exp(tile - highest[:, None]), axis=1) + jnp.sum(
        times * jnp.exp(taken - highest[:, None]), axis=1
    )
    lse = highest + jnp.log(sumexp)
    tile_cols = jnp.arange(blk_count * rows_dev, dtype=jnp.int32)
    own = tile_cols[None, :] == (blk_index * rows_dev + local_rows)[:, None]
    positive = jnp.sum(jnp.where(own, tile, 0.0), axis=1)
    loss_part = jnp.sum(query_weight * (lse - positive))
    mean_loss = lax.psum(loss_part, ("blk", "dp")) / (rows_dev * blk_count * dp_count)
    coefs = (rescale * query_weight)[:, None]
    tile_coef = (coefs * (jnp.exp(tile - lse[:, None]) - own.astype(jnp.float32))).astype(
        jnp.bfloat16
    )
    one_coef = (coefs * jnp.exp(taken - lse[:, None])).astype(jnp.bfloat16)
    pool_coef = (times * one_coef.astype(jnp.float32)).astype(jnp.bfloat16)
    query_grads = jnp.dot(tile_coef, group_passages, preferred_element_type=jnp.float32) + jnp.dot(
        pool_coef, pool_passages, preferred_element_type=jnp.float32
    )
    back_tile = lax.all_to_all(
        tile_coef.T.reshape(blk_count, rows_dev, rows_dev), "blk", 0, 0, tiled=True
    )
    back_pool = lax.all_to_all(
        pool_coef.T.reshape(dp_count, rows_dev, rows_dev), "dp", 0, 0, tiled=True
    )
    back_tile = back_tile.transpose(1, 0, 2).reshape(rows_dev, -1)
    back_pool = back_pool.transpose(1, 0, 2).reshape(rows_dev, -1)
    passage_grads = jnp.dot(back_tile, group_queries, preferred_element_type=jnp.float32) + jnp.dot(
        back_pool, pool_queries, preferred_element_type=jnp.float32
    )
    return (query_grads, passage_grads, mean_loss)


MESH = pl.DeviceIdType.MESH
HALVES = 2
CHUNKS = 8
AHEAD = 2
FIRST = 3
LAST = 5


def line_kernel(
    blk_count,
    q_ref,
    p_ref,
    ids_ref,
    weight_ref,
    qg_ref,
    pg_ref,
    loss_ref,
    pp,
    pq,
    gp,
    gq,
    r_out,
    r_in,
    lp,
    le,
    lt,
    pc,
    tc,
    tt,
    cm,
    ce,
    tr,
    meta,
    hb,
    st_out,
    st_in,
    loss_dp,
    loss_blk,
    s_pin,
    s_pout,
    s_psib,
    r_p,
    r_psib,
    s_qin,
    s_qsib,
    r_q,
    r_qsib,
    s_r,
    r_r,
    s_gp,
    r_gp,
    s_gq,
    r_gq,
    s_t,
    r_t,
    s_m,
    r_m,
    s_h,
    r_h,
    s_st,
    r_st,
    s_ld,
    r_ld,
    s_lb,
    r_lb,
):
    b = lax.axis_index("blk")
    d = lax.axis_index("dp")
    rows, width = q_ref.shape
    half = rows // HALVES
    part = width // CHUNKS
    hard_count = ids_ref.shape[0]
    rescale = 4.0 / math.sqrt(width)
    f32, bf16 = jnp.float32, jnp.bfloat16
    z = lax.div(d, 2)
    c = lax.rem(d, 2)
    o = 1 - c
    side = lax.div(z, 2)
    se, sm = 3 * side, 1 + side
    mp, ep = 3 - sm, 3 - se
    sib = (b, 2 * z + o)
    inner = (b, 2 * jnp.where(z == se, sm, mp) + c)
    outer = (b, 2 * se + c)

    barrier = pltpu.get_barrier_semaphore()
    peers = [(b, lax.rem(d + i, 8)) for i in range(1, 8)]
    others = [lax.rem(b + i, blk_count) for i in range(1, blk_count)]
    peers += [(other, d) for other in others]
    for peer in peers:
        pl.semaphore_signal(barrier, inc=1, device_id=peer, device_id_type=MESH)

    def core_rows(core):
        return pl.ds(pl.multiple_of(core * rows, rows), rows)

    pp[z, core_rows(c), :] = p_ref[...]
    pq[z, core_rows(c), :] = q_ref[...]
    gp[core_rows(b), :] = p_ref[...]
    gq[core_rows(b), :] = q_ref[...]
    meta[d, 0:hard_count, :] = ids_ref[...].astype(f32)
    meta[d, hard_count:, :] = jnp.broadcast_to(weight_ref[...], (8, rows))
    pl.semaphore_wait(barrier, len(peers))

    def remote(src, dst, send_sem, recv_sem, device):
        return pltpu.make_async_remote_copy(
            src_ref=src,
            dst_ref=dst,
            send_sem=send_sem,
            recv_sem=recv_sem,
            device_id=device,
            device_id_type=MESH,
        )

    def p_slot(zz, core, h):
        return pp.at[zz, pl.ds(pl.multiple_of(core * rows + h * half, half), half), :]

    def q_slot(zz, core, j):
        return pq.at[zz, core_rows(core), pl.ds(j * part, part)]

    def p_src(zz, h, own):
        return p_ref.at[pl.ds(h * half, half), :] if own else p_slot(zz, c, h)

    def q_src(zz, j, own):
        return q_ref.at[:, pl.ds(j * part, part)] if own else q_slot(zz, c, j)

    def p_in(zz, h, own=False):
        return remote(p_src(zz, h, own), p_slot(zz, c, h), s_pin.at[zz, h], r_p.at[zz, h], inner)

    def p_out(zz, h, own=False):
        return remote(p_src(zz, h, own), p_slot(zz, c, h), s_pout.at[zz, h], r_p.at[zz, h], outer)

    def p_sib(zz, h, own=False):
        return remote(p_src(zz, h, own), p_slot(zz, c, h), s_psib.at[zz, h], r_psib.at[zz, h], sib)

    def q_in(zz, j, own=False):
        return remote(q_src(zz, j, own), q_slot(zz, c, j), s_qin.at[zz, j], r_q.at[zz, j], inner)

    def q_sib(zz, j, own=False):
        return remote(q_src(zz, j, own), q_slot(zz, c, j), s_qsib.at[zz, j], r_qsib.at[zz, j], sib)

    def wait_p(zz, h):
        slot = p_slot(zz, c, h)
        remote(slot, slot, s_pin.at[zz, h], r_p.at[zz, h], inner).wait_recv()

    def wait_psib(zz):
        for h in range(HALVES):
            slot = p_slot(zz, o, h)
            remote(slot, slot, s_psib.at[zz, h], r_psib.at[zz, h], sib).wait_recv()

    def wait_q(zz, j):
        slot = q_slot(zz, c, j)
        remote(slot, slot, s_qin.at[zz, j], r_q.at[zz, j], inner).wait_recv()

    def wait_qsib(zz, j):
        slot = q_slot(zz, o, j)
        remote(slot, slot, s_qsib.at[zz, j], r_qsib.at[zz, j], sib).wait_recv()

    def r_copy(j):
        cols = pl.ds(j * part, part)
        return remote(r_out.at[:, cols], r_in.at[:, cols], s_r.at[j], r_r.at[j], outer)

    xn = b + 1 - 2 * lax.rem(b, 2)
    yn = b + 2 - 4 * lax.div(b, 2)
    near = (xn, yn)

    def half_rows(owner, h):
        return pl.ds(pl.multiple_of(owner * rows + h * half, half), half)

    def g_copy(own, buf, s_sem, r_sem, n, h):
        src = own.at[pl.ds(h * half, half), :]
        dst = buf.at[half_rows(b, h), :]
        return remote(src, dst, s_sem.at[n, h], r_sem.at[b, h], (near[n], d))

    def g_relay(buf, s_sem, r_sem, n):
        h = 1 - n
        slot = buf.at[half_rows(near[1 - n], h), :]
        return remote(slot, slot, s_sem.at[2, n], r_sem.at[near[1 - n], h], (near[n], d))

    def g_wait(buf, s_sem, r_sem, owner, h):
        slot = buf.at[half_rows(owner, h), :]
        remote(slot, slot, s_sem.at[0, h], r_sem.at[owner, h], (xn, d)).wait_recv()

    def g_start(own, buf, s_sem, r_sem):
        for h in range(HALVES):
            g_copy(own, buf, s_sem, r_sem, 0, h).start()
            g_copy(own, buf, s_sem, r_sem, 1, 1 - h).start()

    def g_forward(buf, s_sem, r_sem):
        g_wait(buf, s_sem, r_sem, xn, 0)
        g_relay(buf, s_sem, r_sem, 1).start()
        g_wait(buf, s_sem, r_sem, yn, 1)
        g_relay(buf, s_sem, r_sem, 0).start()

    def g_finish(buf, s_sem, r_sem):
        g_wait(buf, s_sem, r_sem, xn, 1)
        g_wait(buf, s_sem, r_sem, yn, 0)
        g_wait(buf, s_sem, r_sem, 3 - b, 0)
        g_wait(buf, s_sem, r_sem, 3 - b, 1)

    def g_sent(own, buf, s_sem, r_sem):
        for n in range(2):
            for h in range(HALVES):
                g_copy(own, buf, s_sem, r_sem, n, h).wait_send()
            g_relay(buf, s_sem, r_sem, n).wait_send()

    def t_copy(i):
        return remote(
            tt.at[others[i]], tr.at[:, core_rows(b)], s_t.at[i], r_t.at[b], (others[i], d)
        )

    def ld_copy(i):
        return remote(loss_dp.at[d], loss_dp.at[d], s_ld.at[i], r_ld.at[d], peers[i])

    def lb_copy(i):
        return remote(loss_blk.at[b], loss_blk.at[b], s_lb.at[i], r_lb.at[b], (others[i], d))

    def wait_t():
        for i, other in enumerate(others):
            slot = tr.at[:, core_rows(other)]
            remote(slot, slot, s_t.at[i], r_t.at[other], (other, d)).wait_recv()

    def m_copy(host):
        return remote(meta.at[d], meta.at[d], s_m.at[host - 2], r_m.at[d], (b, host))

    def wait_m(sender):
        slot = meta.at[sender]
        remote(slot, slot, s_m.at[0], r_m.at[sender], (b, sender)).wait_recv()

    hosts = (2 * sm + o, 2 * mp + c, 2 * mp + o)
    end_dev = 2 * se + c

    def h_copy(n, owner, mine):
        slot = hb.at[owner]
        return remote(slot, slot, s_h.at[mine, n], r_h.at[owner], (b, hosts[n]))

    def wait_h(owner):
        slot = hb.at[owner]
        remote(slot, slot, s_h.at[0, 0], r_h.at[owner], sib).wait_recv()

    def st_copy():
        return remote(st_out, st_in, s_st.at[0], r_st.at[0], inner)

    nt = (((1,), (1,)), ((), ()))
    step = min(512, width)

    def pool_logits(zz):
        def body(k, acc):
            cols = pl.ds(pl.multiple_of(k * step, step), step)
            return acc + lax.dot_general(
                q_ref[:, cols], pp[zz, :, cols], nt, preferred_element_type=f32
            )

        zero = jnp.zeros((rows, 2 * rows), f32)
        lp[zz] = lax.fori_loop(0, width // step, body, zero) * rescale

    def end_logits():
        @pl.loop(0, 4)
        def _(zz):
            def body(k, acc):
                cols = pl.ds(pl.multiple_of(k * step, step), step)
                return acc + lax.dot_general(
                    pq[se, core_rows(c), cols], pp[zz, :, cols], nt, preferred_element_type=f32
                )

            zero = jnp.zeros((rows, 2 * rows), f32)
            le[zz] = lax.fori_loop(0, width // step, body, zero) * rescale

    def tile_logits():
        def body(k, acc):
            cols = pl.ds(pl.multiple_of(k * step, step), step)
            return acc + lax.dot_general(
                q_ref[:, cols], gp[:, cols], nt, preferred_element_type=f32
            )

        zero = jnp.zeros((rows, blk_count * rows), f32)
        lt[...] = lax.fori_loop(0, width // step, body, zero) * rescale

    def columns_of(device):
        rest = jnp.zeros((rows - hard_count - 8, rows), f32)
        return jnp.concatenate([meta[device], rest], axis=0).T

    lanes = lax.broadcasted_iota(jnp.int32, (rows, rows), 1)

    def pool_ids(zz):
        iota = lax.broadcasted_iota(jnp.int32, (rows, 2 * rows), 1)
        return (iota + zz * 2 * rows).astype(f32)

    def hard_logits(logits, info):
        found = jnp.full((rows, rows), -jnp.inf, f32)
        for k in range(hard_count):
            total = jnp.zeros((rows, 2 * rows), f32)
            for zz in range(4):
                total += jnp.where(pool_ids(zz) == info[:, k : k + 1], logits[zz], 0.0)
            found = jnp.where(lanes == k, jnp.sum(total, axis=1, keepdims=True), found)
        return found

    def row_stats():
        top = jnp.max(lt[...], axis=1, keepdims=True)
        return top, jnp.sum(jnp.exp(lt[...] - top), axis=1, keepdims=True)

    def hard_softmax(logits, info, top, total):
        found = hard_logits(logits, info)
        highest = jnp.maximum(top, jnp.max(found, axis=1, keepdims=True))
        sumexp = total * jnp.exp(top - highest)
        sumexp += jnp.sum(jnp.exp(found - highest), axis=1, keepdims=True)
        lse = highest + jnp.log(sumexp)
        coefs = rescale * info[:, hard_count : hard_count + 1]
        return lse, (coefs * jnp.exp(found - lse)).astype(bf16).astype(f32)

    def query_side(info, lse, hard):
        weight = info[:, hard_count : hard_count + 1]
        tile = lt[...]
        row = lax.broadcasted_iota(jnp.int32, tile.shape, 0) + b * rows
        own = lax.broadcasted_iota(jnp.int32, tile.shape, 1) == row
        coef = rescale * weight * (jnp.exp(tile - lse) - own.astype(f32))
        tc[...] = coef.astype(bf16)
        for g in range(blk_count):
            tt[g] = coef[:, g * rows : (g + 1) * rows].T.astype(bf16)
        for i in range(len(others)):
            t_copy(i).start()
        tr[:, core_rows(b)] = tt[b]
        positive = jnp.sum(jnp.where(own, tile, 0.0), axis=1, keepdims=True)
        loss = jnp.sum(weight * (lse - positive), axis=0, keepdims=True)
        loss_dp[d] = jnp.broadcast_to(loss, (8, 128))
        for i in range(7):
            ld_copy(i).start()
        for zz in range(4):
            total = jnp.zeros((rows, 2 * rows), f32)
            for k in range(hard_count):
                total += jnp.where(pool_ids(zz) == info[:, k : k + 1], hard[:, k : k + 1], 0.0)
            pc[zz] = total.astype(bf16)

    def passage_side(buf, owner):
        iota = lax.broadcasted_iota(jnp.int32, (rows, rows), 0)
        ids = (iota + owner * rows).astype(f32)

        @pl.loop(0, 4)
        def _(zz):
            for core in range(2):
                dev = 2 * zz + core
                total = jnp.zeros((rows, rows), f32)
                for k in range(hard_count):
                    hit = meta[dev, k : k + 1, :] == ids
                    total += jnp.where(hit, hb[dev, k : k + 1, :], 0.0)
                buf[zz, :, core * rows : (core + 1) * rows] = total.astype(bf16)

    def query_grads():
        @pl.loop(0, CHUNKS)
        def _(j):
            cols = pl.ds(pl.multiple_of(j * part, part), part)
            acc = jnp.dot(tc[...], gp[:, cols], preferred_element_type=f32)
            for zz in range(4):
                acc += jnp.dot(pc[zz], pp[zz, :, cols], preferred_element_type=f32)
            qg_ref[:, cols] = acc

    def group():
        g_finish(gp, s_gp, r_gp)
        g_start(q_ref, gq, s_gq, r_gq)
        tile_logits()

    def tile_grads():
        g_finish(gq, s_gq, r_gq)
        wait_t()

        @pl.loop(0, CHUNKS)
        def _(j):
            cols = pl.ds(pl.multiple_of(j * part, part), part)
            pg_ref[:, cols] = jnp.dot(tr[...], gq[:, cols], preferred_element_type=f32)

    @pl.when(z == sm)
    def _():
        for h in range(HALVES):
            p_in(sm, h, True).start()
        g_start(p_ref, gp, s_gp, r_gp)
        for h in range(HALVES):
            p_out(sm, h, True).start()
            p_sib(sm, h, True).start()
        for host in range(2, 6):

            @pl.when(host != d)
            def _():
                m_copy(host).start()

        wait_psib(sm)
        pool_logits(sm)
        g_forward(gp, s_gp, r_gp)
        for h in range(HALVES):
            wait_p(se, h)
            p_in(se, h).start()
            p_sib(se, h).start()
            wait_p(mp, h)
            p_out(mp, h).start()
            p_sib(mp, h).start()
        for j in range(CHUNKS):
            q_sib(sm, j, True).start()
        for i in range(7):
            wait_m(peers[i][1])
        wait_psib(se)
        pool_logits(se)
        wait_psib(mp)
        pool_logits(mp)
        group()
        top, total = row_stats()
        for h in range(HALVES):
            wait_p(ep, h)
            p_out(ep, h).start()
            p_sib(ep, h).start()
        for j in range(AHEAD):
            q_in(sm, j, True).start()
        for j in range(CHUNKS):
            wait_q(se, j)
            if j < AHEAD:
                q_in(se, j).start()
            q_sib(se, j).start()
        wait_psib(ep)
        pool_logits(ep)
        info = columns_of(d)
        lse, hard = hard_softmax(lp, info, top, total)
        hb[d] = hard.T[0:hard_count, :]
        for n in range(3):
            h_copy(n, d, 0).start()
        end_logits()
        remote(st_in, st_in, s_st.at[0], r_st.at[0], outer).wait_recv()
        end_hard = hard_softmax(le, columns_of(end_dev), st_in[:, 0:1], st_in[:, 1:2])[1]
        hb[end_dev] = end_hard.T[0:hard_count, :]
        for n in range(3):
            h_copy(n, end_dev, 1).start()

        def q_step(j):
            wait_q(mp, j)
            q_sib(mp, j).start()
            wait_q(ep, j)
            q_sib(ep, j).start()
            if j + AHEAD < CHUNKS:
                q_in(sm, j + AHEAD, True).start()
                q_in(se, j + AHEAD).start()

        def end_grads(j):
            for zz in (se, sm, mp, ep):
                wait_qsib(zz, j)
            cols = pl.ds(j * part, part)
            acc = jnp.zeros((rows, part), f32)
            for zz in range(4):
                acc += jnp.dot(ce[zz], pq[zz, :, cols], preferred_element_type=f32)
            r_out[:, cols] = acc.astype(bf16)
            r_copy(j).start()

        def own_grads(j):
            cols = pl.ds(j * part, part)
            acc = pg_ref[:, cols]
            for zz in range(4):
                acc += jnp.dot(cm[zz], pq[zz, :, cols], preferred_element_type=f32)
            pg_ref[:, cols] = acc

        q_step(0)
        query_side(info, lse, hard)
        g_forward(gq, s_gq, r_gq)
        query_grads()
        for j in range(1, CHUNKS):
            q_step(j)
            if j == FIRST:
                for dev in (2 * sm + o, 2 * se + o, 2 * mp, 2 * mp + 1, 2 * ep, 2 * ep + 1):
                    wait_h(dev)
                passage_side(ce, end_dev)
                for i in range(FIRST):
                    end_grads(i)
                passage_side(cm, d)
            if j >= FIRST:
                end_grads(j)
            if j == LAST:
                tile_grads()
                for i in range(LAST):
                    own_grads(i)
            if j >= LAST:
                own_grads(j)

        for h in range(HALVES):
            p_in(sm, h, True).wait_send()
            p_out(sm, h, True).wait_send()
            p_sib(sm, h, True).wait_send()
            p_in(se, h).wait_send()
            p_sib(se, h).wait_send()
            p_out(mp, h).wait_send()
            p_sib(mp, h).wait_send()
            p_out(ep, h).wait_send()
            p_sib(ep, h).wait_send()
        for j in range(CHUNKS):
            q_in(sm, j, True).wait_send()
            q_in(se, j).wait_send()
            q_sib(sm, j, True).wait_send()
            q_sib(se, j).wait_send()
            q_sib(mp, j).wait_send()
            q_sib(ep, j).wait_send()
            r_copy(j).wait_send()
        for n in range(3):
            h_copy(n, d, 0).wait_send()
            h_copy(n, end_dev, 1).wait_send()

    @pl.when(z == se)
    def _():
        for h in range(HALVES):
            p_in(se, h, True).start()
        g_start(p_ref, gp, s_gp, r_gp)
        for h in range(HALVES):
            p_sib(se, h, True).start()
        for host in range(2, 6):
            m_copy(host).start()
        wait_psib(se)
        pool_logits(se)
        g_forward(gp, s_gp, r_gp)
        for h in range(HALVES):
            p_in(se, h, True).wait_send()
        for j in range(CHUNKS):
            q_in(se, j, True).start()

        def receive(zz, h):
            wait_p(zz, h)
            p_sib(zz, h).start()

        receive(sm, 0)
        receive(sm, 1)
        wait_psib(sm)
        pool_logits(sm)
        group()
        top, total = row_stats()
        st_out[...] = jnp.where(lanes == 0, top, total)
        st_copy().start()
        receive(mp, 0)
        receive(mp, 1)
        wait_psib(mp)
        pool_logits(mp)
        receive(ep, 0)
        g_forward(gq, s_gq, r_gq)
        receive(ep, 1)
        wait_psib(ep)
        pool_logits(ep)
        info = columns_of(d)
        lse, hard = hard_softmax(lp, info, top, total)
        query_side(info, lse, hard)
        query_grads()
        tile_grads()
        for j in range(CHUNKS):
            cols = pl.ds(j * part, part)
            r_slot = r_in.at[:, cols]
            remote(r_slot, r_slot, s_r.at[j], r_r.at[j], inner).wait_recv()
            pg_ref[:, cols] += r_in[:, cols].astype(f32)
        st_copy().wait_send()
        for h in range(HALVES):
            p_sib(se, h, True).wait_send()
            for zz in (sm, mp, ep):
                p_sib(zz, h).wait_send()
        for j in range(CHUNKS):
            q_in(se, j, True).wait_send()

    for i in range(7):
        peer = peers[i][1]
        slot = loss_dp.at[peer]
        remote(slot, slot, s_ld.at[i], r_ld.at[peer], peers[i]).wait_recv()
    total = loss_dp[0]
    for s in range(1, 8):
        total = total + loss_dp[s]
    loss_blk[b] = total
    for i in range(len(others)):
        lb_copy(i).start()
    for i, other in enumerate(others):
        slot = loss_blk.at[other]
        remote(slot, slot, s_lb.at[i], r_lb.at[other], (other, d)).wait_recv()
    total = loss_blk[0]
    for g in range(1, blk_count):
        total = total + loss_blk[g]
    loss_ref[0, 0] = jnp.max(total) / (rows * blk_count * 8)
    for i in range(len(others)):
        t_copy(i).wait_send()
        lb_copy(i).wait_send()
    for i in range(7):
        ld_copy(i).wait_send()
    g_sent(p_ref, gp, s_gp, r_gp)
    g_sent(q_ref, gq, s_gq, r_gq)
    for host in range(2, 6):

        @pl.when(host != d)
        def _():
            m_copy(host).wait_send()


def on_line(queries, passages, hard_ids, query_weight):
    rows, width = queries.shape
    blk_count = lax.axis_size("blk")
    hard_count = hard_ids.shape[1]
    bf16, f32 = jnp.bfloat16, jnp.float32
    dma = pltpu.SemaphoreType.DMA
    vmem = pl.BlockSpec(memory_space=pltpu.VMEM)
    query_grads, passage_grads, loss = pl.pallas_call(
        functools.partial(line_kernel, blk_count),
        out_shape=(
            jax.ShapeDtypeStruct((rows, width), f32),
            jax.ShapeDtypeStruct((rows, width), f32),
            jax.ShapeDtypeStruct((1, 1), f32),
        ),
        in_specs=[vmem] * 4,
        out_specs=(vmem, vmem, pl.BlockSpec(memory_space=pltpu.SMEM)),
        scratch_shapes=[
            pltpu.VMEM((4, 2 * rows, width), bf16),
            pltpu.VMEM((4, 2 * rows, width), bf16),
            pltpu.VMEM((blk_count * rows, width), bf16),
            pltpu.VMEM((blk_count * rows, width), bf16),
            pltpu.VMEM((rows, width), bf16),
            pltpu.VMEM((rows, width), bf16),
            pltpu.VMEM((4, rows, 2 * rows), f32),
            pltpu.VMEM((4, rows, 2 * rows), f32),
            pltpu.VMEM((rows, blk_count * rows), f32),
            pltpu.VMEM((4, rows, 2 * rows), bf16),
            pltpu.VMEM((rows, blk_count * rows), bf16),
            pltpu.VMEM((blk_count, rows, rows), bf16),
            pltpu.VMEM((4, rows, 2 * rows), bf16),
            pltpu.VMEM((4, rows, 2 * rows), bf16),
            pltpu.VMEM((rows, blk_count * rows), bf16),
            pltpu.VMEM((8, hard_count + 8, rows), f32),
            pltpu.VMEM((8, hard_count, rows), f32),
            pltpu.VMEM((rows, rows), f32),
            pltpu.VMEM((rows, rows), f32),
            pltpu.VMEM((8, 8, 128), f32),
            pltpu.VMEM((blk_count, 8, 128), f32),
        ]
        + [dma((4, HALVES))] * 5
        + [dma((4, CHUNKS))] * 4
        + [dma((CHUNKS,))] * 2
        + [dma((3, HALVES)), dma((blk_count, HALVES))] * 2
        + [dma((blk_count,))] * 2
        + [dma((4,)), dma((8,))]
        + [dma((2, 3)), dma((8,))]
        + [dma((1,))] * 2
        + [dma((8,))] * 2
        + [dma((blk_count,))] * 2,
        compiler_params=pltpu.CompilerParams(
            collective_id=0, has_side_effects=True, vmem_limit_bytes=44 * 1024 * 1024
        ),
    )(queries, passages, hard_ids.T, query_weight[None, :])
    return (query_grads, passage_grads, loss.reshape(()))


def solution(mesh):
    small = mesh.shape["dp"] == 8 and mesh.shape["blk"] == 4
    return jax.shard_map(
        on_line if small else pooled,
        mesh=mesh,
        in_specs=(
            P(("blk", "dp"), None),
            P(("blk", "dp"), None),
            P(("blk", "dp"), None),
            P(("blk", "dp")),
        ),
        out_specs=(P(("blk", "dp"), None), P(("blk", "dp"), None), P()),
        check_vma=False,
    )
```

```python
import functools
import math

import jax
import jax.numpy as jnp
from jax import lax
from jax.experimental import pallas as pl
from jax.experimental.pallas import tpu as pltpu
from jax.sharding import PartitionSpec as P


def pooled(queries, passages, hard_ids, query_weight):
    rows_dev = queries.shape[0]
    width = queries.shape[1]
    hard_count = hard_ids.shape[1]
    rescale = 4.0 / math.sqrt(width)
    blk_count = lax.axis_size("blk")
    dp_count = lax.axis_size("dp")
    blk_index = lax.axis_index("blk")
    local_rows = jnp.arange(rows_dev, dtype=jnp.int32)
    pool_passages = lax.all_gather(passages, "dp", axis=0, tiled=True)
    group_passages = lax.all_gather(passages, "blk", axis=0, tiled=True)
    pool_queries = lax.all_gather(queries, "dp", axis=0, tiled=True)
    group_queries = lax.all_gather(queries, "blk", axis=0, tiled=True)
    contract = (((1,), (1,)), ((), ()))
    tile = lax.dot_general(queries, group_passages, contract, preferred_element_type=jnp.float32)
    tile = tile * rescale
    pool = lax.dot_general(queries, pool_passages, contract, preferred_element_type=jnp.float32)
    pool = pool * rescale
    pool_cols = jnp.arange(dp_count * rows_dev, dtype=jnp.int32)
    times = jnp.zeros(pool.shape, jnp.float32)
    for k in range(hard_count):
        times = times + (hard_ids[:, k : k + 1] == pool_cols[None, :]).astype(jnp.float32)
    taken = jnp.where(times > 0.0, pool, -jnp.inf)
    highest = jnp.maximum(jnp.max(tile, axis=1), jnp.max(taken, axis=1))
    sumexp = jnp.sum(jnp.exp(tile - highest[:, None]), axis=1) + jnp.sum(
        times * jnp.exp(taken - highest[:, None]), axis=1
    )
    lse = highest + jnp.log(sumexp)
    tile_cols = jnp.arange(blk_count * rows_dev, dtype=jnp.int32)
    own = tile_cols[None, :] == (blk_index * rows_dev + local_rows)[:, None]
    positive = jnp.sum(jnp.where(own, tile, 0.0), axis=1)
    loss_part = jnp.sum(query_weight * (lse - positive))
    mean_loss = lax.psum(loss_part, ("blk", "dp")) / (rows_dev * blk_count * dp_count)
    coefs = (rescale * query_weight)[:, None]
    tile_coef = (coefs * (jnp.exp(tile - lse[:, None]) - own.astype(jnp.float32))).astype(
        jnp.bfloat16
    )
    one_coef = (coefs * jnp.exp(taken - lse[:, None])).astype(jnp.bfloat16)
    pool_coef = (times * one_coef.astype(jnp.float32)).astype(jnp.bfloat16)
    query_grads = jnp.dot(tile_coef, group_passages, preferred_element_type=jnp.float32) + jnp.dot(
        pool_coef, pool_passages, preferred_element_type=jnp.float32
    )
    back_tile = lax.all_to_all(
        tile_coef.T.reshape(blk_count, rows_dev, rows_dev), "blk", 0, 0, tiled=True
    )
    back_pool = lax.all_to_all(
        pool_coef.T.reshape(dp_count, rows_dev, rows_dev), "dp", 0, 0, tiled=True
    )
    back_tile = back_tile.transpose(1, 0, 2).reshape(rows_dev, -1)
    back_pool = back_pool.transpose(1, 0, 2).reshape(rows_dev, -1)
    passage_grads = jnp.dot(back_tile, group_queries, preferred_element_type=jnp.float32) + jnp.dot(
        back_pool, pool_queries, preferred_element_type=jnp.float32
    )
    return (query_grads, passage_grads, mean_loss)


MESH = pl.DeviceIdType.MESH
HALVES = 2
CHUNKS = 8
AHEAD = 3
FIRST = 3
LAST = 5


def line_kernel(
    blk_count,
    q_ref,
    p_ref,
    ids_ref,
    weight_ref,
    qg_ref,
    pg_ref,
    loss_ref,
    pp,
    pq,
    gp,
    gq,
    r_out,
    r_in,
    lp,
    le,
    lt,
    pc,
    tc,
    tt,
    cm,
    ce,
    tr,
    meta,
    hb,
    st_out,
    st_in,
    loss_dp,
    loss_blk,
    s_pin,
    s_pout,
    s_psib,
    r_p,
    r_psib,
    s_qin,
    s_qsib,
    r_q,
    r_qsib,
    s_r,
    r_r,
    s_gp,
    r_gp,
    s_gq,
    r_gq,
    s_t,
    r_t,
    s_m,
    r_m,
    s_h,
    r_h,
    s_st,
    r_st,
    s_ld,
    r_ld,
    s_lb,
    r_lb,
    ids_v,
    weight_v,
    s_own,
):
    b = lax.axis_index("blk")
    d = lax.axis_index("dp")
    rows, width = q_ref.shape
    half = rows // HALVES
    part = width // CHUNKS
    hard_count = ids_ref.shape[0]
    rescale = 4.0 / math.sqrt(width)
    f32, bf16 = jnp.float32, jnp.bfloat16
    z = lax.div(d, 2)
    c = lax.rem(d, 2)
    o = 1 - c
    side = lax.div(z, 2)
    se, sm = 3 * side, 1 + side
    mp, ep = 3 - sm, 3 - se
    sib = (b, 2 * z + o)
    inner = (b, 2 * jnp.where(z == se, sm, mp) + c)
    outer = (b, 2 * se + c)

    barrier = pltpu.get_barrier_semaphore()
    peers = [(b, lax.rem(d + i, 8)) for i in range(1, 8)]
    others = [lax.rem(b + i, blk_count) for i in range(1, blk_count)]
    peers += [(other, d) for other in others]
    for peer in peers:
        pl.semaphore_signal(barrier, inc=1, device_id=peer, device_id_type=MESH)

    def core_rows(core):
        return pl.ds(pl.multiple_of(core * rows, rows), rows)

    local = [
        pltpu.make_async_copy(src, dst, s_own.at[i])
        for i, (src, dst) in enumerate(
            (
                (ids_ref, ids_v),
                (weight_ref, weight_v),
                (p_ref, pp.at[z, core_rows(c), :]),
                (q_ref, gq.at[core_rows(b), :]),
                (p_ref, gp.at[core_rows(b), :]),
                (q_ref, pq.at[z, core_rows(c), :]),
            )
        )
    ]
    for copy in local:
        copy.start()
    pl.semaphore_wait(barrier, len(peers))

    def take_own():
        for copy in local:
            copy.wait()
        meta[d, 0:hard_count, :] = ids_v[...].astype(f32)
        meta[d, hard_count:, :] = jnp.broadcast_to(weight_v[...], (8, rows))

    def remote(src, dst, send_sem, recv_sem, device):
        return pltpu.make_async_remote_copy(
            src_ref=src,
            dst_ref=dst,
            send_sem=send_sem,
            recv_sem=recv_sem,
            device_id=device,
            device_id_type=MESH,
        )

    def p_slot(zz, core, h):
        return pp.at[zz, pl.ds(pl.multiple_of(core * rows + h * half, half), half), :]

    def q_slot(zz, core, j):
        return pq.at[zz, core_rows(core), pl.ds(j * part, part)]

    def p_src(zz, h, own):
        return p_ref.at[pl.ds(h * half, half), :] if own else p_slot(zz, c, h)

    def q_src(zz, j, own):
        return q_ref.at[:, pl.ds(j * part, part)] if own else q_slot(zz, c, j)

    def p_in(zz, h, own=False):
        return remote(p_src(zz, h, own), p_slot(zz, c, h), s_pin.at[zz, h], r_p.at[zz, h], inner)

    def p_out(zz, h, own=False):
        return remote(p_src(zz, h, own), p_slot(zz, c, h), s_pout.at[zz, h], r_p.at[zz, h], outer)

    def p_sib(zz, h, own=False):
        return remote(p_src(zz, h, own), p_slot(zz, c, h), s_psib.at[zz, h], r_psib.at[zz, h], sib)

    def q_in(zz, j, own=False):
        return remote(q_src(zz, j, own), q_slot(zz, c, j), s_qin.at[zz, j], r_q.at[zz, j], inner)

    def q_sib(zz, j, own=False):
        return remote(q_src(zz, j, own), q_slot(zz, c, j), s_qsib.at[zz, j], r_qsib.at[zz, j], sib)

    def wait_p(zz, h):
        slot = p_slot(zz, c, h)
        remote(slot, slot, s_pin.at[zz, h], r_p.at[zz, h], inner).wait_recv()

    def wait_psib(zz):
        for h in range(HALVES):
            slot = p_slot(zz, o, h)
            remote(slot, slot, s_psib.at[zz, h], r_psib.at[zz, h], sib).wait_recv()

    def wait_q(zz, j):
        slot = q_slot(zz, c, j)
        remote(slot, slot, s_qin.at[zz, j], r_q.at[zz, j], inner).wait_recv()

    def wait_qsib(zz, j):
        slot = q_slot(zz, o, j)
        remote(slot, slot, s_qsib.at[zz, j], r_qsib.at[zz, j], sib).wait_recv()

    def r_copy(j):
        cols = pl.ds(j * part, part)
        return remote(r_out.at[:, cols], r_in.at[:, cols], s_r.at[j], r_r.at[j], outer)

    xn = b + 1 - 2 * lax.rem(b, 2)
    yn = b + 2 - 4 * lax.div(b, 2)
    near = (xn, yn)

    def half_rows(owner, h):
        return pl.ds(pl.multiple_of(owner * rows + h * half, half), half)

    def g_copy(own, buf, s_sem, r_sem, n, h):
        src = own.at[pl.ds(h * half, half), :]
        dst = buf.at[half_rows(b, h), :]
        return remote(src, dst, s_sem.at[n, h], r_sem.at[b, h], (near[n], d))

    def g_relay(buf, s_sem, r_sem, n):
        h = 1 - n
        slot = buf.at[half_rows(near[1 - n], h), :]
        return remote(slot, slot, s_sem.at[2, n], r_sem.at[near[1 - n], h], (near[n], d))

    def g_wait(buf, s_sem, r_sem, owner, h):
        slot = buf.at[half_rows(owner, h), :]
        remote(slot, slot, s_sem.at[0, h], r_sem.at[owner, h], (xn, d)).wait_recv()

    def g_start(own, buf, s_sem, r_sem):
        for h in range(HALVES):
            g_copy(own, buf, s_sem, r_sem, 0, h).start()
            g_copy(own, buf, s_sem, r_sem, 1, 1 - h).start()

    def g_forward(buf, s_sem, r_sem):
        g_wait(buf, s_sem, r_sem, xn, 0)
        g_relay(buf, s_sem, r_sem, 1).start()
        g_wait(buf, s_sem, r_sem, yn, 1)
        g_relay(buf, s_sem, r_sem, 0).start()

    def g_finish(buf, s_sem, r_sem):
        g_wait(buf, s_sem, r_sem, xn, 1)
        g_wait(buf, s_sem, r_sem, yn, 0)
        g_wait(buf, s_sem, r_sem, 3 - b, 0)
        g_wait(buf, s_sem, r_sem, 3 - b, 1)

    def g_sent(own, buf, s_sem, r_sem):
        for n in range(2):
            for h in range(HALVES):
                g_copy(own, buf, s_sem, r_sem, n, h).wait_send()
            g_relay(buf, s_sem, r_sem, n).wait_send()

    def t_copy(i):
        return remote(
            tt.at[others[i]], tr.at[:, core_rows(b)], s_t.at[i], r_t.at[b], (others[i], d)
        )

    def ld_copy(i):
        return remote(loss_dp.at[d], loss_dp.at[d], s_ld.at[i], r_ld.at[d], peers[i])

    def lb_copy(i):
        return remote(loss_blk.at[b], loss_blk.at[b], s_lb.at[i], r_lb.at[b], (others[i], d))

    def wait_t():
        for i, other in enumerate(others):
            slot = tr.at[:, core_rows(other)]
            remote(slot, slot, s_t.at[i], r_t.at[other], (other, d)).wait_recv()

    def m_copy(host):
        return remote(meta.at[d], meta.at[d], s_m.at[host - 2], r_m.at[d], (b, host))

    def wait_m(sender):
        slot = meta.at[sender]
        remote(slot, slot, s_m.at[0], r_m.at[sender], (b, sender)).wait_recv()

    hosts = (2 * sm + o, 2 * mp + c, 2 * mp + o)
    end_dev = 2 * se + c

    def h_copy(n, owner, mine):
        slot = hb.at[owner]
        return remote(slot, slot, s_h.at[mine, n], r_h.at[owner], (b, hosts[n]))

    def wait_h(owner):
        slot = hb.at[owner]
        remote(slot, slot, s_h.at[0, 0], r_h.at[owner], sib).wait_recv()

    def st_copy():
        return remote(st_out, st_in, s_st.at[0], r_st.at[0], inner)

    nt = (((1,), (1,)), ((), ()))
    step = min(512, width)

    def pool_logits(zz):
        def body(k, acc):
            cols = pl.ds(pl.multiple_of(k * step, step), step)
            return acc + lax.dot_general(
                gq[core_rows(b), cols], pp[zz, :, cols], nt, preferred_element_type=f32
            )

        zero = jnp.zeros((rows, 2 * rows), f32)
        lp[zz] = lax.fori_loop(0, width // step, body, zero) * rescale

    def end_logits():
        @pl.loop(0, 4)
        def _(zz):
            def body(k, acc):
                cols = pl.ds(pl.multiple_of(k * step, step), step)
                return acc + lax.dot_general(
                    pq[se, core_rows(c), cols], pp[zz, :, cols], nt, preferred_element_type=f32
                )

            zero = jnp.zeros((rows, 2 * rows), f32)
            le[zz] = lax.fori_loop(0, width // step, body, zero) * rescale

    def tile_logits():
        def body(k, acc):
            cols = pl.ds(pl.multiple_of(k * step, step), step)
            return acc + lax.dot_general(
                gq[core_rows(b), cols], gp[:, cols], nt, preferred_element_type=f32
            )

        zero = jnp.zeros((rows, blk_count * rows), f32)
        lt[...] = lax.fori_loop(0, width // step, body, zero) * rescale

    def columns_of(device):
        rest = jnp.zeros((rows - hard_count - 8, rows), f32)
        return jnp.concatenate([meta[device], rest], axis=0).T

    lanes = lax.broadcasted_iota(jnp.int32, (rows, rows), 1)

    def pool_ids(zz):
        iota = lax.broadcasted_iota(jnp.int32, (rows, 2 * rows), 1)
        return (iota + zz * 2 * rows).astype(f32)

    def hard_logits(logits, info):
        found = jnp.full((rows, rows), -jnp.inf, f32)
        for k in range(hard_count):
            total = jnp.zeros((rows, 2 * rows), f32)
            for zz in range(4):
                total += jnp.where(pool_ids(zz) == info[:, k : k + 1], logits[zz], 0.0)
            found = jnp.where(lanes == k, jnp.sum(total, axis=1, keepdims=True), found)
        return found

    def row_stats():
        top = jnp.max(lt[...], axis=1, keepdims=True)
        return top, jnp.sum(jnp.exp(lt[...] - top), axis=1, keepdims=True)

    def hard_softmax(logits, info, top, total):
        found = hard_logits(logits, info)
        highest = jnp.maximum(top, jnp.max(found, axis=1, keepdims=True))
        sumexp = total * jnp.exp(top - highest)
        sumexp += jnp.sum(jnp.exp(found - highest), axis=1, keepdims=True)
        lse = highest + jnp.log(sumexp)
        coefs = rescale * info[:, hard_count : hard_count + 1]
        return lse, (coefs * jnp.exp(found - lse)).astype(bf16).astype(f32)

    def query_side(info, lse, hard):
        weight = info[:, hard_count : hard_count + 1]
        tile = lt[...]
        row = lax.broadcasted_iota(jnp.int32, tile.shape, 0) + b * rows
        own = lax.broadcasted_iota(jnp.int32, tile.shape, 1) == row
        coef = rescale * weight * (jnp.exp(tile - lse) - own.astype(f32))
        tc[...] = coef.astype(bf16)
        for g in range(blk_count):
            tt[g] = coef[:, g * rows : (g + 1) * rows].T.astype(bf16)
        for i in range(len(others)):
            t_copy(i).start()
        tr[:, core_rows(b)] = tt[b]
        positive = jnp.sum(jnp.where(own, tile, 0.0), axis=1, keepdims=True)
        loss = jnp.sum(weight * (lse - positive), axis=0, keepdims=True)
        loss_dp[d] = jnp.broadcast_to(loss, (8, 128))
        for i in range(7):
            ld_copy(i).start()
        for zz in range(4):
            total = jnp.zeros((rows, 2 * rows), f32)
            for k in range(hard_count):
                total += jnp.where(pool_ids(zz) == info[:, k : k + 1], hard[:, k : k + 1], 0.0)
            pc[zz] = total.astype(bf16)

    def passage_side(buf, owner):
        iota = lax.broadcasted_iota(jnp.int32, (rows, rows), 0)
        ids = (iota + owner * rows).astype(f32)

        @pl.loop(0, 4)
        def _(zz):
            for core in range(2):
                dev = 2 * zz + core
                total = jnp.zeros((rows, rows), f32)
                for k in range(hard_count):
                    hit = meta[dev, k : k + 1, :] == ids
                    total += jnp.where(hit, hb[dev, k : k + 1, :], 0.0)
                buf[zz, :, core * rows : (core + 1) * rows] = total.astype(bf16)

    def query_grads():
        @pl.loop(0, CHUNKS)
        def _(j):
            cols = pl.ds(pl.multiple_of(j * part, part), part)
            acc = jnp.dot(tc[...], gp[:, cols], preferred_element_type=f32)
            for zz in range(4):
                acc += jnp.dot(pc[zz], pp[zz, :, cols], preferred_element_type=f32)
            qg_ref[:, cols] = acc

    def group():
        g_finish(gp, s_gp, r_gp)
        g_start(q_ref, gq, s_gq, r_gq)
        tile_logits()

    def tile_grads():
        g_finish(gq, s_gq, r_gq)
        wait_t()

        @pl.loop(0, CHUNKS)
        def _(j):
            cols = pl.ds(pl.multiple_of(j * part, part), part)
            pg_ref[:, cols] = jnp.dot(tr[...], gq[:, cols], preferred_element_type=f32)

    @pl.when(z == sm)
    def _():
        for h in range(HALVES):
            p_in(sm, h, True).start()
        g_start(p_ref, gp, s_gp, r_gp)
        for h in range(HALVES):
            p_out(sm, h, True).start()
            p_sib(sm, h, True).start()
        take_own()
        for host in range(2, 6):

            @pl.when(host != d)
            def _():
                m_copy(host).start()

        wait_psib(sm)
        pool_logits(sm)
        g_forward(gp, s_gp, r_gp)
        for h in range(HALVES):
            wait_p(se, h)
            p_in(se, h).start()
            p_sib(se, h).start()
            wait_p(mp, h)
            p_out(mp, h).start()
            p_sib(mp, h).start()
        for j in range(CHUNKS):
            q_sib(sm, j, True).start()
        for i in range(7):
            wait_m(peers[i][1])
        wait_psib(se)
        pool_logits(se)
        wait_psib(mp)
        pool_logits(mp)
        group()
        top, total = row_stats()
        for h in range(HALVES):
            wait_p(ep, h)
            p_out(ep, h).start()
            p_sib(ep, h).start()
            if h == 0:
                q_in(sm, 0, True).start()
        for j in range(CHUNKS):
            if 0 < j < AHEAD:
                q_in(sm, j, True).start()
            wait_q(se, j)
            if j < AHEAD:
                q_in(se, j).start()
            q_sib(se, j).start()
        def q_step(j):
            wait_q(mp, j)
            q_sib(mp, j).start()
            wait_q(ep, j)
            q_sib(ep, j).start()
            if j + AHEAD < CHUNKS:
                q_in(sm, j + AHEAD, True).start()
                q_in(se, j + AHEAD).start()

        wait_psib(ep)
        pool_logits(ep)
        info = columns_of(d)
        lse, hard = hard_softmax(lp, info, top, total)
        hb[d] = hard.T[0:hard_count, :]
        for n in range(3):
            h_copy(n, d, 0).start()
        end_logits()
        q_step(0)
        remote(st_in, st_in, s_st.at[0], r_st.at[0], outer).wait_recv()
        end_hard = hard_softmax(le, columns_of(end_dev), st_in[:, 0:1], st_in[:, 1:2])[1]
        hb[end_dev] = end_hard.T[0:hard_count, :]
        for n in range(3):
            h_copy(n, end_dev, 1).start()

        def end_grads(j):
            for zz in (se, sm, mp, ep):
                wait_qsib(zz, j)
            cols = pl.ds(j * part, part)
            acc = jnp.zeros((rows, part), f32)
            for zz in range(4):
                acc += jnp.dot(ce[zz], pq[zz, :, cols], preferred_element_type=f32)
            r_out[:, cols] = acc.astype(bf16)
            r_copy(j).start()

        def own_grads(j):
            cols = pl.ds(j * part, part)
            acc = pg_ref[:, cols]
            for zz in range(4):
                acc += jnp.dot(cm[zz], pq[zz, :, cols], preferred_element_type=f32)
            pg_ref[:, cols] = acc

        q_step(1)
        query_side(info, lse, hard)
        g_forward(gq, s_gq, r_gq)
        q_step(2)
        query_grads()
        for j in range(3, CHUNKS):
            q_step(j)
            if j == FIRST:
                for dev in (2 * sm + o, 2 * se + o, 2 * mp, 2 * mp + 1, 2 * ep, 2 * ep + 1):
                    wait_h(dev)
                passage_side(ce, end_dev)
                for i in range(FIRST):
                    end_grads(i)
                passage_side(cm, d)
            if j >= FIRST:
                end_grads(j)
            if j == LAST:
                tile_grads()
                for i in range(LAST):
                    own_grads(i)
            if j >= LAST:
                own_grads(j)

        for h in range(HALVES):
            p_in(sm, h, True).wait_send()
            p_out(sm, h, True).wait_send()
            p_sib(sm, h, True).wait_send()
            p_in(se, h).wait_send()
            p_sib(se, h).wait_send()
            p_out(mp, h).wait_send()
            p_sib(mp, h).wait_send()
            p_out(ep, h).wait_send()
            p_sib(ep, h).wait_send()
        for j in range(CHUNKS):
            q_in(sm, j, True).wait_send()
            q_in(se, j).wait_send()
            q_sib(sm, j, True).wait_send()
            q_sib(se, j).wait_send()
            q_sib(mp, j).wait_send()
            q_sib(ep, j).wait_send()
            r_copy(j).wait_send()
        for n in range(3):
            h_copy(n, d, 0).wait_send()
            h_copy(n, end_dev, 1).wait_send()

    @pl.when(z == se)
    def _():
        for h in range(HALVES):
            p_in(se, h, True).start()
        g_start(p_ref, gp, s_gp, r_gp)
        for h in range(HALVES):
            p_sib(se, h, True).start()
        take_own()
        for host in range(2, 6):
            m_copy(host).start()
        wait_psib(se)
        pool_logits(se)
        g_forward(gp, s_gp, r_gp)
        for h in range(HALVES):
            p_in(se, h, True).wait_send()
        for j in range(CHUNKS):
            q_in(se, j, True).start()

        def receive(zz, h):
            wait_p(zz, h)
            p_sib(zz, h).start()

        receive(sm, 0)
        receive(sm, 1)
        wait_psib(sm)
        pool_logits(sm)
        group()
        top, total = row_stats()
        st_out[...] = jnp.where(lanes == 0, top, total)
        st_copy().start()
        receive(mp, 0)
        receive(mp, 1)
        wait_psib(mp)
        pool_logits(mp)
        receive(ep, 0)
        g_forward(gq, s_gq, r_gq)
        receive(ep, 1)
        wait_psib(ep)
        pool_logits(ep)
        info = columns_of(d)
        lse, hard = hard_softmax(lp, info, top, total)
        query_side(info, lse, hard)
        query_grads()
        tile_grads()
        for j in range(CHUNKS):
            cols = pl.ds(j * part, part)
            r_slot = r_in.at[:, cols]
            remote(r_slot, r_slot, s_r.at[j], r_r.at[j], inner).wait_recv()
            pg_ref[:, cols] += r_in[:, cols].astype(f32)
        st_copy().wait_send()
        for h in range(HALVES):
            p_sib(se, h, True).wait_send()
            for zz in (sm, mp, ep):
                p_sib(zz, h).wait_send()
        for j in range(CHUNKS):
            q_in(se, j, True).wait_send()

    for i in range(7):
        peer = peers[i][1]
        slot = loss_dp.at[peer]
        remote(slot, slot, s_ld.at[i], r_ld.at[peer], peers[i]).wait_recv()
    total = loss_dp[0]
    for s in range(1, 8):
        total = total + loss_dp[s]
    loss_blk[b] = total
    for i in range(len(others)):
        lb_copy(i).start()
    for i, other in enumerate(others):
        slot = loss_blk.at[other]
        remote(slot, slot, s_lb.at[i], r_lb.at[other], (other, d)).wait_recv()
    total = loss_blk[0]
    for g in range(1, blk_count):
        total = total + loss_blk[g]
    loss_ref[0, 0] = jnp.max(total) / (rows * blk_count * 8)
    for i in range(len(others)):
        t_copy(i).wait_send()
        lb_copy(i).wait_send()
    for i in range(7):
        ld_copy(i).wait_send()
    g_sent(p_ref, gp, s_gp, r_gp)
    g_sent(q_ref, gq, s_gq, r_gq)
    for host in range(2, 6):

        @pl.when(host != d)
        def _():
            m_copy(host).wait_send()


def on_line(queries, passages, hard_ids, query_weight):
    rows, width = queries.shape
    blk_count = lax.axis_size("blk")
    hard_count = hard_ids.shape[1]
    bf16, f32 = jnp.bfloat16, jnp.float32
    dma = pltpu.SemaphoreType.DMA
    vmem = pl.BlockSpec(memory_space=pltpu.VMEM)
    query_grads, passage_grads, loss = pl.pallas_call(
        functools.partial(line_kernel, blk_count),
        out_shape=(
            jax.ShapeDtypeStruct((rows, width), f32),
            jax.ShapeDtypeStruct((rows, width), f32),
            jax.ShapeDtypeStruct((1, 1), f32),
        ),
        in_specs=[pl.BlockSpec(memory_space=pltpu.HBM)] * 4,
        out_specs=(vmem, vmem, pl.BlockSpec(memory_space=pltpu.SMEM)),
        scratch_shapes=[
            pltpu.VMEM((4, 2 * rows, width), bf16),
            pltpu.VMEM((4, 2 * rows, width), bf16),
            pltpu.VMEM((blk_count * rows, width), bf16),
            pltpu.VMEM((blk_count * rows, width), bf16),
            pltpu.VMEM((rows, width), bf16),
            pltpu.VMEM((rows, width), bf16),
            pltpu.VMEM((4, rows, 2 * rows), f32),
            pltpu.VMEM((4, rows, 2 * rows), f32),
            pltpu.VMEM((rows, blk_count * rows), f32),
            pltpu.VMEM((4, rows, 2 * rows), bf16),
            pltpu.VMEM((rows, blk_count * rows), bf16),
            pltpu.VMEM((blk_count, rows, rows), bf16),
            pltpu.VMEM((4, rows, 2 * rows), bf16),
            pltpu.VMEM((4, rows, 2 * rows), bf16),
            pltpu.VMEM((rows, blk_count * rows), bf16),
            pltpu.VMEM((8, hard_count + 8, rows), f32),
            pltpu.VMEM((8, hard_count, rows), f32),
            pltpu.VMEM((rows, rows), f32),
            pltpu.VMEM((rows, rows), f32),
            pltpu.VMEM((8, 8, 128), f32),
            pltpu.VMEM((blk_count, 8, 128), f32),
        ]
        + [dma((4, HALVES))] * 5
        + [dma((4, CHUNKS))] * 4
        + [dma((CHUNKS,))] * 2
        + [dma((3, HALVES)), dma((blk_count, HALVES))] * 2
        + [dma((blk_count,))] * 2
        + [dma((4,)), dma((8,))]
        + [dma((2, 3)), dma((8,))]
        + [dma((1,))] * 2
        + [dma((8,))] * 2
        + [dma((blk_count,))] * 2
        + [pltpu.VMEM((hard_count, rows), jnp.int32), pltpu.VMEM((1, rows), f32), dma((6,))],
        compiler_params=pltpu.CompilerParams(
            collective_id=0, has_side_effects=True, vmem_limit_bytes=44 * 1024 * 1024
        ),
    )(queries, passages, hard_ids.T, query_weight[None, :])
    return (query_grads, passage_grads, loss.reshape(()))


def solution(mesh):
    small = mesh.shape["dp"] == 8 and mesh.shape["blk"] == 4
    return jax.shard_map(
        on_line if small else pooled,
        mesh=mesh,
        in_specs=(
            P(("blk", "dp"), None),
            P(("blk", "dp"), None),
            P(("blk", "dp"), None),
            P(("blk", "dp")),
        ),
        out_specs=(P(("blk", "dp"), None), P(("blk", "dp"), None), P()),
        check_vma=False,
    )
```

```python
import functools
import math

import jax
import jax.numpy as jnp
from jax import lax
from jax.experimental import pallas as pl
from jax.experimental.pallas import tpu as pltpu
from jax.sharding import PartitionSpec as P


def pooled(queries, passages, hard_ids, query_weight):
    rows_dev = queries.shape[0]
    width = queries.shape[1]
    hard_count = hard_ids.shape[1]
    rescale = 4.0 / math.sqrt(width)
    blk_count = lax.axis_size("blk")
    dp_count = lax.axis_size("dp")
    blk_index = lax.axis_index("blk")
    local_rows = jnp.arange(rows_dev, dtype=jnp.int32)
    pool_passages = lax.all_gather(passages, "dp", axis=0, tiled=True)
    group_passages = lax.all_gather(passages, "blk", axis=0, tiled=True)
    pool_queries = lax.all_gather(queries, "dp", axis=0, tiled=True)
    group_queries = lax.all_gather(queries, "blk", axis=0, tiled=True)
    contract = (((1,), (1,)), ((), ()))
    tile = lax.dot_general(queries, group_passages, contract, preferred_element_type=jnp.float32)
    tile = tile * rescale
    pool = lax.dot_general(queries, pool_passages, contract, preferred_element_type=jnp.float32)
    pool = pool * rescale
    pool_cols = jnp.arange(dp_count * rows_dev, dtype=jnp.int32)
    times = jnp.zeros(pool.shape, jnp.float32)
    for k in range(hard_count):
        times = times + (hard_ids[:, k : k + 1] == pool_cols[None, :]).astype(jnp.float32)
    taken = jnp.where(times > 0.0, pool, -jnp.inf)
    highest = jnp.maximum(jnp.max(tile, axis=1), jnp.max(taken, axis=1))
    sumexp = jnp.sum(jnp.exp(tile - highest[:, None]), axis=1) + jnp.sum(
        times * jnp.exp(taken - highest[:, None]), axis=1
    )
    lse = highest + jnp.log(sumexp)
    tile_cols = jnp.arange(blk_count * rows_dev, dtype=jnp.int32)
    own = tile_cols[None, :] == (blk_index * rows_dev + local_rows)[:, None]
    positive = jnp.sum(jnp.where(own, tile, 0.0), axis=1)
    loss_part = jnp.sum(query_weight * (lse - positive))
    mean_loss = lax.psum(loss_part, ("blk", "dp")) / (rows_dev * blk_count * dp_count)
    coefs = (rescale * query_weight)[:, None]
    tile_coef = (coefs * (jnp.exp(tile - lse[:, None]) - own.astype(jnp.float32))).astype(
        jnp.bfloat16
    )
    one_coef = (coefs * jnp.exp(taken - lse[:, None])).astype(jnp.bfloat16)
    pool_coef = (times * one_coef.astype(jnp.float32)).astype(jnp.bfloat16)
    query_grads = jnp.dot(tile_coef, group_passages, preferred_element_type=jnp.float32) + jnp.dot(
        pool_coef, pool_passages, preferred_element_type=jnp.float32
    )
    back_tile = lax.all_to_all(
        tile_coef.T.reshape(blk_count, rows_dev, rows_dev), "blk", 0, 0, tiled=True
    )
    back_pool = lax.all_to_all(
        pool_coef.T.reshape(dp_count, rows_dev, rows_dev), "dp", 0, 0, tiled=True
    )
    back_tile = back_tile.transpose(1, 0, 2).reshape(rows_dev, -1)
    back_pool = back_pool.transpose(1, 0, 2).reshape(rows_dev, -1)
    passage_grads = jnp.dot(back_tile, group_queries, preferred_element_type=jnp.float32) + jnp.dot(
        back_pool, pool_queries, preferred_element_type=jnp.float32
    )
    return (query_grads, passage_grads, mean_loss)


MESH = pl.DeviceIdType.MESH
HALVES = 2
CHUNKS = 8
STEP = CHUNKS // 8
BEGIN = 2 * STEP
AHEAD = 3 * STEP
FIRST = 3 * STEP
LAST = 5 * STEP


def line_kernel(
    blk_count,
    q_ref,
    p_ref,
    ids_ref,
    weight_ref,
    qg_ref,
    pg_ref,
    loss_ref,
    pp,
    pq,
    gp,
    gq,
    r_out,
    r_in,
    lp,
    le,
    lt,
    pc,
    tc,
    tt,
    cm,
    ce,
    tr,
    meta,
    hb,
    st_out,
    st_in,
    loss_dp,
    loss_blk,
    s_pin,
    s_pout,
    s_psib,
    r_p,
    r_psib,
    s_qin,
    s_qsib,
    r_q,
    r_qsib,
    s_r,
    r_r,
    s_gp,
    r_gp,
    s_gq,
    r_gq,
    s_t,
    r_t,
    s_m,
    r_m,
    s_h,
    r_h,
    s_st,
    r_st,
    s_ld,
    r_ld,
    s_lb,
    r_lb,
    ids_v,
    weight_v,
    s_own,
):
    b = lax.axis_index("blk")
    d = lax.axis_index("dp")
    rows, width = q_ref.shape
    half = rows // HALVES
    part = width // CHUNKS
    hard_count = ids_ref.shape[0]
    rescale = 4.0 / math.sqrt(width)
    f32, bf16 = jnp.float32, jnp.bfloat16
    z = lax.div(d, 2)
    c = lax.rem(d, 2)
    o = 1 - c
    side = lax.div(z, 2)
    se, sm = 3 * side, 1 + side
    mp, ep = 3 - sm, 3 - se
    sib = (b, 2 * z + o)
    inner = (b, 2 * jnp.where(z == se, sm, mp) + c)
    outer = (b, 2 * se + c)

    barrier = pltpu.get_barrier_semaphore()
    peers = [(b, lax.rem(d + i, 8)) for i in range(1, 8)]
    others = [lax.rem(b + i, blk_count) for i in range(1, blk_count)]
    peers += [(other, d) for other in others]
    for peer in peers:
        pl.semaphore_signal(barrier, inc=1, device_id=peer, device_id_type=MESH)

    def core_rows(core):
        return pl.ds(pl.multiple_of(core * rows, rows), rows)

    local = [
        pltpu.make_async_copy(src, dst, s_own.at[i])
        for i, (src, dst) in enumerate(
            (
                (ids_ref, ids_v),
                (weight_ref, weight_v),
                (p_ref, pp.at[z, core_rows(c), :]),
                (q_ref, gq.at[core_rows(b), :]),
                (p_ref, gp.at[core_rows(b), :]),
                (q_ref, pq.at[z, core_rows(c), :]),
            )
        )
    ]
    for copy in local:
        copy.start()
    pl.semaphore_wait(barrier, len(peers))

    def take_own():
        for copy in local:
            copy.wait()
        meta[d, 0:hard_count, :] = ids_v[...].astype(f32)
        meta[d, hard_count:, :] = jnp.broadcast_to(weight_v[...], (8, rows))

    def remote(src, dst, send_sem, recv_sem, device):
        return pltpu.make_async_remote_copy(
            src_ref=src,
            dst_ref=dst,
            send_sem=send_sem,
            recv_sem=recv_sem,
            device_id=device,
            device_id_type=MESH,
        )

    def p_slot(zz, core, h):
        return pp.at[zz, pl.ds(pl.multiple_of(core * rows + h * half, half), half), :]

    def q_slot(zz, core, j):
        return pq.at[zz, core_rows(core), pl.ds(j * part, part)]

    def p_src(zz, h, own):
        return p_ref.at[pl.ds(h * half, half), :] if own else p_slot(zz, c, h)

    def q_src(zz, j, own):
        return q_ref.at[:, pl.ds(j * part, part)] if own else q_slot(zz, c, j)

    def p_in(zz, h, own=False):
        return remote(p_src(zz, h, own), p_slot(zz, c, h), s_pin.at[zz, h], r_p.at[zz, h], inner)

    def p_out(zz, h, own=False):
        return remote(p_src(zz, h, own), p_slot(zz, c, h), s_pout.at[zz, h], r_p.at[zz, h], outer)

    def p_sib(zz, h, own=False):
        return remote(p_src(zz, h, own), p_slot(zz, c, h), s_psib.at[zz, h], r_psib.at[zz, h], sib)

    def q_in(zz, j, own=False):
        return remote(q_src(zz, j, own), q_slot(zz, c, j), s_qin.at[zz, j], r_q.at[zz, j], inner)

    def q_sib(zz, j, own=False):
        return remote(q_src(zz, j, own), q_slot(zz, c, j), s_qsib.at[zz, j], r_qsib.at[zz, j], sib)

    def wait_p(zz, h):
        slot = p_slot(zz, c, h)
        remote(slot, slot, s_pin.at[zz, h], r_p.at[zz, h], inner).wait_recv()

    def wait_psib(zz):
        for h in range(HALVES):
            slot = p_slot(zz, o, h)
            remote(slot, slot, s_psib.at[zz, h], r_psib.at[zz, h], sib).wait_recv()

    def wait_q(zz, j):
        slot = q_slot(zz, c, j)
        remote(slot, slot, s_qin.at[zz, j], r_q.at[zz, j], inner).wait_recv()

    def wait_qsib(zz, j):
        slot = q_slot(zz, o, j)
        remote(slot, slot, s_qsib.at[zz, j], r_qsib.at[zz, j], sib).wait_recv()

    def r_copy(j):
        cols = pl.ds(j * part, part)
        return remote(r_out.at[:, cols], r_in.at[:, cols], s_r.at[j], r_r.at[j], outer)

    xn = b + 1 - 2 * lax.rem(b, 2)
    yn = b + 2 - 4 * lax.div(b, 2)
    near = (xn, yn)

    def half_rows(owner, h):
        return pl.ds(pl.multiple_of(owner * rows + h * half, half), half)

    def g_copy(own, buf, s_sem, r_sem, n, h):
        src = own.at[pl.ds(h * half, half), :]
        dst = buf.at[half_rows(b, h), :]
        return remote(src, dst, s_sem.at[n, h], r_sem.at[b, h], (near[n], d))

    def g_relay(buf, s_sem, r_sem, n):
        h = 1 - n
        slot = buf.at[half_rows(near[1 - n], h), :]
        return remote(slot, slot, s_sem.at[2, n], r_sem.at[near[1 - n], h], (near[n], d))

    def g_wait(buf, s_sem, r_sem, owner, h):
        slot = buf.at[half_rows(owner, h), :]
        remote(slot, slot, s_sem.at[0, h], r_sem.at[owner, h], (xn, d)).wait_recv()

    def g_start(own, buf, s_sem, r_sem):
        for h in range(HALVES):
            g_copy(own, buf, s_sem, r_sem, 0, h).start()
            g_copy(own, buf, s_sem, r_sem, 1, 1 - h).start()

    def g_forward(buf, s_sem, r_sem):
        g_wait(buf, s_sem, r_sem, xn, 0)
        g_relay(buf, s_sem, r_sem, 1).start()
        g_wait(buf, s_sem, r_sem, yn, 1)
        g_relay(buf, s_sem, r_sem, 0).start()

    def g_finish(buf, s_sem, r_sem):
        g_wait(buf, s_sem, r_sem, xn, 1)
        g_wait(buf, s_sem, r_sem, yn, 0)
        g_wait(buf, s_sem, r_sem, 3 - b, 0)
        g_wait(buf, s_sem, r_sem, 3 - b, 1)

    def g_sent(own, buf, s_sem, r_sem):
        for n in range(2):
            for h in range(HALVES):
                g_copy(own, buf, s_sem, r_sem, n, h).wait_send()
            g_relay(buf, s_sem, r_sem, n).wait_send()

    def t_copy(i):
        return remote(
            tt.at[others[i]], tr.at[:, core_rows(b)], s_t.at[i], r_t.at[b], (others[i], d)
        )

    def ld_copy(i):
        return remote(loss_dp.at[d], loss_dp.at[d], s_ld.at[i], r_ld.at[d], peers[i])

    def lb_copy(i):
        return remote(loss_blk.at[b], loss_blk.at[b], s_lb.at[i], r_lb.at[b], (others[i], d))

    def wait_t():
        for i, other in enumerate(others):
            slot = tr.at[:, core_rows(other)]
            remote(slot, slot, s_t.at[i], r_t.at[other], (other, d)).wait_recv()

    def m_copy(host):
        return remote(meta.at[d], meta.at[d], s_m.at[host - 2], r_m.at[d], (b, host))

    def wait_m(sender):
        slot = meta.at[sender]
        remote(slot, slot, s_m.at[0], r_m.at[sender], (b, sender)).wait_recv()

    hosts = (2 * sm + o, 2 * mp + c, 2 * mp + o)
    end_dev = 2 * se + c

    def h_copy(n, owner, mine):
        slot = hb.at[owner]
        return remote(slot, slot, s_h.at[mine, n], r_h.at[owner], (b, hosts[n]))

    def wait_h(owner):
        slot = hb.at[owner]
        remote(slot, slot, s_h.at[0, 0], r_h.at[owner], sib).wait_recv()

    def st_copy():
        return remote(st_out, st_in, s_st.at[0], r_st.at[0], inner)

    nt = (((1,), (1,)), ((), ()))
    step = min(512, width)

    def pool_logits(zz):
        def body(k, acc):
            cols = pl.ds(pl.multiple_of(k * step, step), step)
            return acc + lax.dot_general(
                gq[core_rows(b), cols], pp[zz, :, cols], nt, preferred_element_type=f32
            )

        zero = jnp.zeros((rows, 2 * rows), f32)
        lp[zz] = lax.fori_loop(0, width // step, body, zero) * rescale

    def end_part(j):
        cols = pl.ds(j * part, part)
        left = pq[se, core_rows(c), cols]
        for zz in (se, sm, mp):
            term = lax.dot_general(left, pp[zz, :, cols], nt, preferred_element_type=f32)
            le[zz] = term * rescale if j == 0 else le[zz] + term * rescale

    def both_logits(zz):
        def body(k, acc):
            cols = pl.ds(pl.multiple_of(k * step, step), step)
            left = jnp.concatenate([gq[core_rows(b), cols], pq[se, core_rows(c), cols]], axis=0)
            return acc + lax.dot_general(left, pp[zz, :, cols], nt, preferred_element_type=f32)

        zero = jnp.zeros((2 * rows, 2 * rows), f32)
        out = lax.fori_loop(0, width // step, body, zero) * rescale
        lp[zz] = out[:rows]
        le[zz] = out[rows:]

    def tile_logits():
        def body(k, acc):
            cols = pl.ds(pl.multiple_of(k * step, step), step)
            return acc + lax.dot_general(
                gq[core_rows(b), cols], gp[:, cols], nt, preferred_element_type=f32
            )

        zero = jnp.zeros((rows, blk_count * rows), f32)
        lt[...] = lax.fori_loop(0, width // step, body, zero) * rescale

    def columns_of(device):
        rest = jnp.zeros((rows - hard_count - 8, rows), f32)
        return jnp.concatenate([meta[device], rest], axis=0).T

    lanes = lax.broadcasted_iota(jnp.int32, (rows, rows), 1)

    def pool_ids(zz):
        iota = lax.broadcasted_iota(jnp.int32, (rows, 2 * rows), 1)
        return (iota + zz * 2 * rows).astype(f32)

    def hard_logits(logits, info):
        found = jnp.full((rows, rows), -jnp.inf, f32)
        for k in range(hard_count):
            total = jnp.zeros((rows, 2 * rows), f32)
            for zz in range(4):
                total += jnp.where(pool_ids(zz) == info[:, k : k + 1], logits[zz], 0.0)
            found = jnp.where(lanes == k, jnp.sum(total, axis=1, keepdims=True), found)
        return found

    def row_stats():
        top = jnp.max(lt[...], axis=1, keepdims=True)
        return top, jnp.sum(jnp.exp(lt[...] - top), axis=1, keepdims=True)

    def hard_softmax(logits, info, top, total):
        found = hard_logits(logits, info)
        highest = jnp.maximum(top, jnp.max(found, axis=1, keepdims=True))
        sumexp = total * jnp.exp(top - highest)
        sumexp += jnp.sum(jnp.exp(found - highest), axis=1, keepdims=True)
        lse = highest + jnp.log(sumexp)
        coefs = rescale * info[:, hard_count : hard_count + 1]
        return lse, (coefs * jnp.exp(found - lse)).astype(bf16).astype(f32)

    def query_side(info, lse, hard):
        weight = info[:, hard_count : hard_count + 1]
        tile = lt[...]
        row = lax.broadcasted_iota(jnp.int32, tile.shape, 0) + b * rows
        own = lax.broadcasted_iota(jnp.int32, tile.shape, 1) == row
        coef = rescale * weight * (jnp.exp(tile - lse) - own.astype(f32))
        tc[...] = coef.astype(bf16)
        for g in range(blk_count):
            tt[g] = coef[:, g * rows : (g + 1) * rows].T.astype(bf16)
        for i in range(len(others)):
            t_copy(i).start()
        tr[:, core_rows(b)] = tt[b]
        positive = jnp.sum(jnp.where(own, tile, 0.0), axis=1, keepdims=True)
        loss = jnp.sum(weight * (lse - positive), axis=0, keepdims=True)
        loss_dp[d] = jnp.broadcast_to(loss, (8, 128))
        for i in range(7):
            ld_copy(i).start()
        for zz in range(4):
            total = jnp.zeros((rows, 2 * rows), f32)
            for k in range(hard_count):
                total += jnp.where(pool_ids(zz) == info[:, k : k + 1], hard[:, k : k + 1], 0.0)
            pc[zz] = total.astype(bf16)

    def passage_side(buf, owner):
        iota = lax.broadcasted_iota(jnp.int32, (rows, rows), 0)
        ids = (iota + owner * rows).astype(f32)

        @pl.loop(0, 4)
        def _(zz):
            for core in range(2):
                dev = 2 * zz + core
                total = jnp.zeros((rows, rows), f32)
                for k in range(hard_count):
                    hit = meta[dev, k : k + 1, :] == ids
                    total += jnp.where(hit, hb[dev, k : k + 1, :], 0.0)
                buf[zz, :, core * rows : (core + 1) * rows] = total.astype(bf16)

    def query_grads():
        @pl.loop(0, CHUNKS)
        def _(j):
            cols = pl.ds(pl.multiple_of(j * part, part), part)
            acc = jnp.dot(tc[...], gp[:, cols], preferred_element_type=f32)
            for zz in range(4):
                acc += jnp.dot(pc[zz], pp[zz, :, cols], preferred_element_type=f32)
            qg_ref[:, cols] = acc

    def group():
        g_finish(gp, s_gp, r_gp)
        g_start(q_ref, gq, s_gq, r_gq)
        tile_logits()

    def tile_grads():
        g_finish(gq, s_gq, r_gq)
        wait_t()

        @pl.loop(0, CHUNKS)
        def _(j):
            cols = pl.ds(pl.multiple_of(j * part, part), part)
            pg_ref[:, cols] = jnp.dot(tr[...], gq[:, cols], preferred_element_type=f32)

    def loss_line():
        for i in range(7):
            peer = peers[i][1]
            slot = loss_dp.at[peer]
            remote(slot, slot, s_ld.at[i], r_ld.at[peer], peers[i]).wait_recv()
        total = loss_dp[0]
        for s in range(1, 8):
            total = total + loss_dp[s]
        loss_blk[b] = total
        for i in range(len(others)):
            lb_copy(i).start()

    def loss_all():
        for i, other in enumerate(others):
            slot = loss_blk.at[other]
            remote(slot, slot, s_lb.at[i], r_lb.at[other], (other, d)).wait_recv()
        total = loss_blk[0]
        for g in range(1, blk_count):
            total = total + loss_blk[g]
        loss_ref[0, 0] = jnp.max(total) / (rows * blk_count * 8)

    @pl.when(z == sm)
    def _():
        for h in range(HALVES):
            p_in(sm, h, True).start()
        g_start(p_ref, gp, s_gp, r_gp)
        for h in range(HALVES):
            p_out(sm, h, True).start()
            p_sib(sm, h, True).start()
        take_own()
        for host in range(2, 6):

            @pl.when(host != d)
            def _():
                m_copy(host).start()

        wait_psib(sm)
        pool_logits(sm)
        g_forward(gp, s_gp, r_gp)
        for h in range(HALVES):
            wait_p(se, h)
            p_in(se, h).start()
            p_sib(se, h).start()
            wait_p(mp, h)
            p_out(mp, h).start()
            p_sib(mp, h).start()
        for j in range(CHUNKS):
            q_sib(sm, j, True).start()
        for i in range(7):
            wait_m(peers[i][1])
        wait_psib(se)
        pool_logits(se)
        wait_psib(mp)
        pool_logits(mp)
        group()
        top, total = row_stats()
        def take_end(j):
            wait_q(se, j)
            q_sib(se, j).start()
            end_part(j)

        def relay_far(h):
            wait_p(ep, h)
            p_out(ep, h).start()
            p_sib(ep, h).start()

        relay_far(0)
        q_in(sm, 0, True).start()
        for j in range(CHUNKS - STEP):
            take_end(j)
        relay_far(1)
        q_in(se, 0).start()
        for j in range(1, BEGIN):
            q_in(sm, j, True).start()
            q_in(se, j).start()
        for j in range(CHUNKS - STEP, CHUNKS):
            take_end(j)
        def q_step(j):
            wait_q(mp, j)
            q_sib(mp, j).start()
            wait_q(ep, j)
            q_sib(ep, j).start()
            if j >= STEP and j + AHEAD < CHUNKS:
                q_in(sm, j + AHEAD, True).start()
                q_in(se, j + AHEAD).start()

        wait_psib(ep)
        both_logits(ep)
        info = columns_of(d)
        lse, hard = hard_softmax(lp, info, top, total)
        hb[d] = hard.T[0:hard_count, :]
        for n in range(3):
            h_copy(n, d, 0).start()
        for j in range(STEP):
            q_step(j)
        remote(st_in, st_in, s_st.at[0], r_st.at[0], outer).wait_recv()
        end_hard = hard_softmax(le, columns_of(end_dev), st_in[:, 0:1], st_in[:, 1:2])[1]
        hb[end_dev] = end_hard.T[0:hard_count, :]
        for n in range(3):
            h_copy(n, end_dev, 1).start()
        for j in range(BEGIN, AHEAD + STEP):
            q_in(sm, j, True).start()
            q_in(se, j).start()

        def end_grads(j):
            for zz in (se, sm, mp, ep):
                wait_qsib(zz, j)
            cols = pl.ds(j * part, part)
            acc = jnp.zeros((rows, part), f32)
            for zz in range(4):
                acc += jnp.dot(ce[zz], pq[zz, :, cols], preferred_element_type=f32)
            r_out[:, cols] = acc.astype(bf16)
            r_copy(j).start()

        def own_grads(j):
            cols = pl.ds(j * part, part)
            acc = pg_ref[:, cols]
            for zz in range(4):
                acc += jnp.dot(cm[zz], pq[zz, :, cols], preferred_element_type=f32)
            pg_ref[:, cols] = acc

        for j in range(STEP, 2 * STEP):
            q_step(j)
        query_side(info, lse, hard)
        g_forward(gq, s_gq, r_gq)
        for j in range(2 * STEP, FIRST):
            q_step(j)
        query_grads()
        for j in range(FIRST, CHUNKS):
            q_step(j)
            if j == FIRST:
                for dev in (2 * sm + o, 2 * se + o, 2 * mp, 2 * mp + 1, 2 * ep, 2 * ep + 1):
                    wait_h(dev)
                passage_side(ce, end_dev)
                for i in range(FIRST):
                    end_grads(i)
                passage_side(cm, d)
            if j >= FIRST:
                end_grads(j)
            if j == LAST:
                tile_grads()
                for i in range(LAST):
                    own_grads(i)
            if j >= LAST:
                own_grads(j)
            if j == CHUNKS - 1 - STEP:
                loss_line()
        loss_all()

        for h in range(HALVES):
            p_in(sm, h, True).wait_send()
            p_out(sm, h, True).wait_send()
            p_sib(sm, h, True).wait_send()
            p_in(se, h).wait_send()
            p_sib(se, h).wait_send()
            p_out(mp, h).wait_send()
            p_sib(mp, h).wait_send()
            p_out(ep, h).wait_send()
            p_sib(ep, h).wait_send()
        for j in range(CHUNKS):
            q_in(sm, j, True).wait_send()
            q_in(se, j).wait_send()
            q_sib(sm, j, True).wait_send()
            q_sib(se, j).wait_send()
            q_sib(mp, j).wait_send()
            q_sib(ep, j).wait_send()
            r_copy(j).wait_send()
        for n in range(3):
            h_copy(n, d, 0).wait_send()
            h_copy(n, end_dev, 1).wait_send()

    @pl.when(z == se)
    def _():
        for h in range(HALVES):
            p_in(se, h, True).start()
        g_start(p_ref, gp, s_gp, r_gp)
        for h in range(HALVES):
            p_sib(se, h, True).start()
        take_own()
        for host in range(2, 6):
            m_copy(host).start()
        wait_psib(se)
        pool_logits(se)
        g_forward(gp, s_gp, r_gp)
        for h in range(HALVES):
            p_in(se, h, True).wait_send()
        for j in range(CHUNKS):
            q_in(se, j, True).start()

        def receive(zz, h):
            wait_p(zz, h)
            p_sib(zz, h).start()

        receive(sm, 0)
        receive(sm, 1)
        wait_psib(sm)
        pool_logits(sm)
        group()
        top, total = row_stats()
        st_out[...] = jnp.where(lanes == 0, top, total)
        st_copy().start()
        receive(mp, 0)
        receive(mp, 1)
        wait_psib(mp)
        pool_logits(mp)
        receive(ep, 0)
        g_forward(gq, s_gq, r_gq)
        receive(ep, 1)
        wait_psib(ep)
        pool_logits(ep)
        info = columns_of(d)
        lse, hard = hard_softmax(lp, info, top, total)
        query_side(info, lse, hard)
        query_grads()
        tile_grads()
        loss_line()
        for j in range(CHUNKS):
            if j == CHUNKS - STEP:
                loss_all()
            cols = pl.ds(j * part, part)
            r_slot = r_in.at[:, cols]
            remote(r_slot, r_slot, s_r.at[j], r_r.at[j], inner).wait_recv()
            pg_ref[:, cols] += r_in[:, cols].astype(f32)
        st_copy().wait_send()
        for h in range(HALVES):
            p_sib(se, h, True).wait_send()
            for zz in (sm, mp, ep):
                p_sib(zz, h).wait_send()
        for j in range(CHUNKS):
            q_in(se, j, True).wait_send()

    for i in range(len(others)):
        t_copy(i).wait_send()
        lb_copy(i).wait_send()
    for i in range(7):
        ld_copy(i).wait_send()
    g_sent(p_ref, gp, s_gp, r_gp)
    g_sent(q_ref, gq, s_gq, r_gq)
    for host in range(2, 6):

        @pl.when(host != d)
        def _():
            m_copy(host).wait_send()


def on_line(queries, passages, hard_ids, query_weight):
    rows, width = queries.shape
    blk_count = lax.axis_size("blk")
    hard_count = hard_ids.shape[1]
    bf16, f32 = jnp.bfloat16, jnp.float32
    dma = pltpu.SemaphoreType.DMA
    vmem = pl.BlockSpec(memory_space=pltpu.VMEM)
    query_grads, passage_grads, loss = pl.pallas_call(
        functools.partial(line_kernel, blk_count),
        out_shape=(
            jax.ShapeDtypeStruct((rows, width), f32),
            jax.ShapeDtypeStruct((rows, width), f32),
            jax.ShapeDtypeStruct((1, 1), f32),
        ),
        in_specs=[pl.BlockSpec(memory_space=pltpu.HBM)] * 4,
        out_specs=(vmem, vmem, pl.BlockSpec(memory_space=pltpu.SMEM)),
        scratch_shapes=[
            pltpu.VMEM((4, 2 * rows, width), bf16),
            pltpu.VMEM((4, 2 * rows, width), bf16),
            pltpu.VMEM((blk_count * rows, width), bf16),
            pltpu.VMEM((blk_count * rows, width), bf16),
            pltpu.VMEM((rows, width), bf16),
            pltpu.VMEM((rows, width), bf16),
            pltpu.VMEM((4, rows, 2 * rows), f32),
            pltpu.VMEM((4, rows, 2 * rows), f32),
            pltpu.VMEM((rows, blk_count * rows), f32),
            pltpu.VMEM((4, rows, 2 * rows), bf16),
            pltpu.VMEM((rows, blk_count * rows), bf16),
            pltpu.VMEM((blk_count, rows, rows), bf16),
            pltpu.VMEM((4, rows, 2 * rows), bf16),
            pltpu.VMEM((4, rows, 2 * rows), bf16),
            pltpu.VMEM((rows, blk_count * rows), bf16),
            pltpu.VMEM((8, hard_count + 8, rows), f32),
            pltpu.VMEM((8, hard_count, rows), f32),
            pltpu.VMEM((rows, rows), f32),
            pltpu.VMEM((rows, rows), f32),
            pltpu.VMEM((8, 8, 128), f32),
            pltpu.VMEM((blk_count, 8, 128), f32),
        ]
        + [dma((4, HALVES))] * 5
        + [dma((4, CHUNKS))] * 4
        + [dma((CHUNKS,))] * 2
        + [dma((3, HALVES)), dma((blk_count, HALVES))] * 2
        + [dma((blk_count,))] * 2
        + [dma((4,)), dma((8,))]
        + [dma((2, 3)), dma((8,))]
        + [dma((1,))] * 2
        + [dma((8,))] * 2
        + [dma((blk_count,))] * 2
        + [pltpu.VMEM((hard_count, rows), jnp.int32), pltpu.VMEM((1, rows), f32), dma((6,))],
        compiler_params=pltpu.CompilerParams(
            collective_id=0, has_side_effects=True, vmem_limit_bytes=44 * 1024 * 1024
        ),
    )(queries, passages, hard_ids.T, query_weight[None, :])
    return (query_grads, passage_grads, loss.reshape(()))


def solution(mesh):
    small = mesh.shape["dp"] == 8 and mesh.shape["blk"] == 4
    return jax.shard_map(
        on_line if small else pooled,
        mesh=mesh,
        in_specs=(
            P(("blk", "dp"), None),
            P(("blk", "dp"), None),
            P(("blk", "dp"), None),
            P(("blk", "dp")),
        ),
        out_specs=(P(("blk", "dp"), None), P(("blk", "dp"), None), P()),
        check_vma=False,
    )
```
